32 devices in a mesh: groups: 2 (over y), pulse: 4 (over z), range: 2 (over x), sub: 2 (over core).
Axes of the slice: x: 2, y: 2, z: 4, core: 2. Of those that a mesh axis runs over, the one named last changes fastest.
Arguments:
- raw_echo: bfloat16 [2, 128, 16384], P(None, ('groups', 'pulse', 'sub'), 'range'), parts along dimension 1, may hold values from -6 to 6
- range_taps: bfloat16 [32, 512, 128], P('pulse'), may hold values from -0.25 to 0.25
- azim_taps: bfloat16 [128, 2048], P(('groups', 'pulse', 'sub')), parts along dimension 0, may hold values from -1 to 1
- tile_col: int32 [128, 1], P(('groups', 'pulse', 'sub')), parts along dimension 0, may hold values from 0 to 1; in each aligned block of 4 rows (0 to 3, 4 to 7, ...) at most 2 rows name the same one
Outputs:
- image: float32 [2, 8192, 4096], P(None, ('groups', 'pulse', 'range', 'sub')), parts along dimension 1
The draws below stay inside these ranges and needn't reach their ends.
There are 2 independent parts, one for each index of `groups`. The reference program is written for one: setup_inputs(seed, part) draws one part's arguments, and reference() takes and returns one part's arrays. A program takes and returns all parts, laid end to end along the dimension named above; an argument that names none is the same for every part. Nothing has to cross between parts.
Inputs may be any that keep to these rules, and one draw needn't show every extreme that they name: `tile_col`: in each aligned block of 4 pulses no tile column is named by more than 2 pulses.
All inputs are finite; a program needn't handle non-finite values.
Results may differ from the reference program's by a relative error of at most 0.008.
Values may be sent and summed in bfloat16 or wider, within the bound.
A program may use at most 64 MiB of HBM per device.

```python
import math
import jax
import jax.numpy as jnp
import numpy as np
from jax import lax

S = 16384
G = 4096
KB = 128
PULSE_DEV = 4
CAP = 2
PULSES = 64
PULSE_SHARD = 8
TILE_COLS = 2
TW = 2048
RBIN = 512
N_PULSE = 4
N_RANGE = 2
N_SUB = 2


def levels(own_key, dims, pieces, smallest, largest):
    loudness, own = 1.0, jax.random.fold_in(own_key, 6)
    for dim, shards_of in pieces:
        steps = jnp.exp(jax.random.uniform(jax.random.fold_in(own, dim), (shards_of,), jnp.float32, smallest / len(pieces), largest / len(pieces)))
        loudness = loudness * jnp.repeat(steps, dims[dim] // shards_of).reshape([-1 if axis == dim else 1 for axis in range(len(dims))])
    return loudness


def deal_out(rng, own, number, rows, amount, top, most, slope):
    order = jax.random.permutation(rng, amount)
    heavy_load, common = shares(amount, rows * top, most, slope, True), shares(amount, rows * top, most, slope, False)
    places = jnp.arange(amount)

    def named(sizes, turn):
        used = int((sizes > 0).sum())
        fixed = max(1, used // 4)
        shifted = fixed + (places - fixed + turn * (used - fixed)) % max(1, amount - fixed)
        return jnp.zeros((amount,), jnp.int32).at[order[jnp.where(places < fixed, places, shifted)]].set(jnp.asarray(sizes, jnp.int32))

    sizes = jnp.where(number % 4 == 0, named(heavy_load, number // 4), named(common, number - number // 4 - 1))
    mixed = jax.random.permutation(jax.random.fold_in(own, 3), amount)
    giver, sink = mixed[0:amount // 2 * 2:2], mixed[1:amount // 2 * 2:2]
    margin = jnp.minimum(sizes[giver] - 1, most - sizes[sink]) // 2
    margin = jnp.where((giver == order[0]) | (sink == order[0]) | (sizes[sink] == 0), 0, jnp.maximum(margin, 0))
    shifted = jax.random.randint(jax.random.fold_in(own, 4), (amount // 2,), 0, 1 << 20) % (margin + 1)
    sizes = sizes.at[giver].add(-shifted).at[sink].add(shifted)
    items = jnp.searchsorted(jnp.cumsum(sizes), jnp.arange(rows * top), side="right").astype(jnp.int32)
    grid = items.reshape(top, rows).T
    grid = grid[jax.random.permutation(jax.random.fold_in(own, 1), rows)]
    turn = jax.random.randint(jax.random.fold_in(own, 2), (rows, 1), 0, top)
    return jnp.take_along_axis(grid, (jnp.arange(top)[None, :] + turn) % top, axis=1)


def shares(count, total, most, lean, full):
    loads = [(1 << 20) // math.isqrt(standing ** lean) + 1 for standing in range(1, count + 1)]
    largest = most if full else min(most, max(-(-total // count), total * loads[0] // sum(loads)))
    least = 1 if total - largest >= count - 1 else 0
    holding, spare = [largest] + [least] * (count - 1), total - largest - least * (count - 1)
    while spare > 0:
        candidates = [i for i in range(1, count) if holding[i] < largest] or [i for i in range(1, count) if holding[i] < most]
        pool, budget = sum([loads[i] for i in candidates]), spare
        for i in candidates:
            more = min(most - holding[i], max(1, budget * loads[i] // pool), spare)
            holding[i] = holding[i] + more
            spare = spare - more
    return np.array(holding)


def noise(rng, extent, spread, most, split=(), kind=jnp.bfloat16):
    drawn = jax.random.normal(rng, extent, jnp.float32) * spread
    if len(split) > 0:
        drawn = levels(rng, extent, split, -0.22, 0.18) * drawn
    return jnp.clip(drawn, min=-most, max=most).astype(kind)


def setup_inputs(seed: int = 0, part: int = 0) -> dict:
    key_list = jax.random.split(jax.random.key(seed), 5)
    part_keys = jax.random.split(jax.random.fold_in(key_list[4], part), 5)
    raw_echo = noise(part_keys[0], (2, PULSES, S), 1.0, 6.0, ((1, 8), (2, 2)))
    range_taps = noise(key_list[1], (G // KB, RBIN, KB), RBIN ** -0.5, 0.25, ((0, 4),))
    azim_taps = noise(part_keys[2], (PULSES, TW), (PULSES // TILE_COLS) ** -0.5, 1.0, ((0, 8),))
    tile_col_keys = jax.random.split(jax.random.fold_in(part_keys[3], 1), PULSES // PULSE_DEV)
    tile_col_turns = jax.random.permutation(jax.random.fold_in(part_keys[3], 3), PULSES // PULSE_DEV)
    tile_col = jax.vmap(lambda own, number: deal_out(jax.random.fold_in(part_keys[3], 2), own, number, PULSE_DEV, TILE_COLS, 1, CAP, 2))(tile_col_keys, tile_col_turns).reshape((PULSES, 1))
    return {"raw_echo": raw_echo, "range_taps": range_taps, "azim_taps": azim_taps, "tile_col": tile_col}


def reference(raw_echo, range_taps, azim_taps, tile_col):
    samples = raw_echo.astype(jnp.float32)
    transformed = jnp.fft.fft(samples[0] + 1j * samples[1], norm="ortho")
    spectrum = jnp.stack([jnp.real(transformed), jnp.imag(transformed)]).astype(jnp.bfloat16)
    blocked = spectrum.reshape(2, PULSES, G // KB, RBIN).astype(jnp.float32)
    highest = lax.Precision.HIGHEST
    ky_rows = jnp.einsum("xpbr,brj->xpbj", blocked, range_taps.astype(jnp.float32), precision=highest)
    ky_rows = ky_rows.reshape(2, PULSES, G).astype(jnp.bfloat16)
    by_half = ky_rows.reshape(2, N_PULSE, N_SUB, PULSE_SHARD, G)
    taps_half = azim_taps.reshape(N_PULSE, N_SUB, PULSE_SHARD, TW)
    cols_half = tile_col[:, 0].reshape(N_PULSE, N_SUB, PULSE_SHARD)
    most_rows = N_PULSE * N_RANGE * CAP
    kspace = jnp.zeros((2, G, G), jnp.float32)
    for half_index in range(N_SUB):
        half_lines = by_half[:, :, half_index].reshape(2, N_PULSE * PULSE_SHARD, G)
        half_taps = taps_half[:, half_index].reshape(N_PULSE * PULSE_SHARD, TW)
        half_cols = cols_half[:, half_index].reshape(N_PULSE * PULSE_SHARD)

        def one_tile(column):
            ranked = jnp.argsort(jnp.where(half_cols == column, 0, 1), stable=True)[:most_rows]
            chosen_lines = half_lines[:, ranked].astype(jnp.float32)
            inside = half_cols[ranked] == column
            chosen_taps = jnp.where(inside[:, None], half_taps[ranked].astype(jnp.float32), jnp.zeros((), jnp.float32))
            return jnp.einsum("xpj,pi->xji", chosen_lines, chosen_taps, precision=highest)

        tiles = lax.map(one_tile, jnp.arange(N_RANGE, dtype=jnp.int32))
        partial_value = jnp.transpose(tiles, (1, 2, 0, 3)).reshape(2, G, G)
        rounded = lax.optimization_barrier(partial_value.astype(jnp.bfloat16))
        kspace = kspace + rounded.astype(jnp.float32)
    pictured = jnp.fft.ifft2(kspace[0] + 1j * kspace[1], norm="ortho")
    return jnp.stack([jnp.real(pictured), jnp.imag(pictured)]).astype(jnp.float32)
```

```python
import functools
import math

import jax
import jax.numpy as jnp
import ml_dtypes
import numpy as np
from jax import lax
from jax.experimental import pallas as pl
from jax.experimental.pallas import tpu as pltpu
from jax.sharding import PartitionSpec as P

CAP = 2


def swapped(block, axis, bit):
    count = lax.axis_size(axis)
    route = []
    for low in range(count):
        high = low | 1 << bit
        if high != low and high < count:
            route += [(low, high), (high, low)]
    return lax.ppermute(block, axis, route)


def as_sent(value):
    return jax.tree.map(lambda a: a.astype(jnp.bfloat16) if a.dtype == jnp.float32 else a, value)


def tables(points, direction):
    indices = jnp.arange(points, dtype=jnp.int32)
    phases = indices[:, None] * indices[None, :] % points
    angles = phases.astype(jnp.float32) * (2.0 * math.pi / points)
    return (jnp.cos(angles), direction * jnp.sin(angles))


def spectral(real_part, imag_part, direction):
    length = real_part.shape[-1]
    outer_len = 1 << (length.bit_length() - 1) // 2
    inner_len = length // outer_len
    leading = real_part.shape[:-1]
    real_part = real_part.reshape(leading + (outer_len, inner_len))
    imag_part = imag_part.reshape(leading + (outer_len, inner_len))
    highest = lax.Precision.HIGHEST
    cos_outer, sin_outer = tables(outer_len, direction)
    mixed_real = jnp.einsum(
        "...nm,nk->...km", real_part, cos_outer, precision=highest
    ) - jnp.einsum("...nm,nk->...km", imag_part, sin_outer, precision=highest)
    mixed_imag = jnp.einsum(
        "...nm,nk->...km", real_part, sin_outer, precision=highest
    ) + jnp.einsum("...nm,nk->...km", imag_part, cos_outer, precision=highest)
    outer_index = jnp.arange(outer_len, dtype=jnp.int32)[:, None]
    inner_index = jnp.arange(inner_len, dtype=jnp.int32)[None, :]
    twists = (outer_index * inner_index % length).astype(jnp.float32) * (2.0 * math.pi / length)
    twist_cos = jnp.cos(twists)
    twist_sin = direction * jnp.sin(twists)
    turned_real = mixed_real * twist_cos - mixed_imag * twist_sin
    turned_imag = mixed_real * twist_sin + mixed_imag * twist_cos
    cos_inner, sin_inner = tables(inner_len, direction)
    final_real = jnp.einsum(
        "...km,mj->...jk", turned_real, cos_inner, precision=highest
    ) - jnp.einsum("...km,mj->...jk", turned_imag, sin_inner, precision=highest)
    final_imag = jnp.einsum(
        "...km,mj->...jk", turned_real, sin_inner, precision=highest
    ) + jnp.einsum("...km,mj->...jk", turned_imag, cos_inner, precision=highest)
    norm_scale = 1.0 / math.sqrt(length)
    return (
        (final_real * norm_scale).reshape(leading + (length,)),
        (final_imag * norm_scale).reshape(leading + (length,)),
    )


def general_body(raw_echo, range_taps, azim_taps, tile_col):
    n_range = lax.axis_size("range")
    n_pulse = lax.axis_size("pulse")
    my_range = lax.axis_index("range")
    my_sub = lax.axis_index("sub")
    shard_pulses = raw_echo.shape[1]
    shard_samples = raw_echo.shape[2]
    per_device = shard_pulses // n_range
    grouped = raw_echo.reshape(2, n_range, per_device, shard_samples)
    pieces = lax.all_to_all(grouped, "range", split_axis=1, concat_axis=3, tiled=True)
    real_out, imag_out = spectral(
        pieces[0].astype(jnp.float32), pieces[1].astype(jnp.float32), -1.0
    )
    spectrum = jnp.stack([real_out, imag_out]).astype(jnp.bfloat16)
    spectrum = spectrum.reshape(2, per_device, shard_samples * n_range)
    band_bins = spectrum.shape[2] // n_pulse
    first_pulse = my_range * per_device
    cols_here = lax.dynamic_slice_in_dim(tile_col[:, 0], first_pulse, per_device)
    taps_here = lax.dynamic_slice_in_dim(azim_taps, first_pulse, per_device, 0)
    position = jnp.arange(per_device, dtype=jnp.int32)
    earlier = position[None, :] < position[:, None]
    same_tile = cols_here[:, None] == cols_here[None, :]
    slot_rank = jnp.sum(jnp.where(earlier & same_tile, 1, 0), axis=1)
    tile_ids = jnp.arange(n_range, dtype=jnp.int32)
    slot_ids = jnp.arange(CAP, dtype=jnp.int32)
    placing = (
        (cols_here[None, None, :] == tile_ids[:, None, None])
        & (slot_rank[None, None, :] == slot_ids[None, :, None])
    ).astype(jnp.bfloat16)
    banded = spectrum.reshape(2, per_device, n_pulse, band_bins)
    send_lines = jnp.einsum(
        "tcq,xqpb->ptcxb", placing, banded, preferred_element_type=jnp.float32
    ).astype(jnp.bfloat16)
    send_taps = jnp.einsum(
        "tcq,qw->tcw", placing, taps_here, preferred_element_type=jnp.float32
    ).astype(jnp.bfloat16)
    tile_width = send_taps.shape[2]
    send_taps = jnp.broadcast_to(send_taps[None], (n_pulse, n_range, CAP, tile_width))
    block_count, block_bins, block_rows = range_taps.shape
    flat_lines = send_lines.reshape(n_pulse * n_range, CAP, 2, band_bins)
    flat_taps = send_taps.reshape(n_pulse * n_range, CAP, tile_width)
    line_block = lax.all_to_all(
        flat_lines, ("pulse", "range"), split_axis=0, concat_axis=0, tiled=True
    )
    tap_block = lax.all_to_all(
        flat_taps, ("pulse", "range"), split_axis=0, concat_axis=0, tiled=True
    )
    blocked = line_block.reshape(line_block.shape[:3] + (block_count, block_bins))
    resampled = jnp.einsum(
        "skxbr,brj->skxbj", blocked, range_taps, preferred_element_type=jnp.float32
    )
    ky_rows = resampled.reshape(line_block.shape[:3] + (block_count * block_rows,)).astype(
        jnp.bfloat16
    )
    band_rows = ky_rows.shape[3]
    slot_total = ky_rows.shape[0] * ky_rows.shape[1]
    slot_lines = ky_rows.reshape(slot_total, 2, band_rows)
    slot_taps = tap_block.reshape(slot_total, tile_width)
    half_width = tile_width // 2
    other_lines, other_taps = swapped((slot_lines, slot_taps), "sub", 0)
    column_start = my_sub * half_width
    my_taps = lax.dynamic_slice_in_dim(slot_taps, column_start, half_width, 1)
    their_taps = lax.dynamic_slice_in_dim(other_taps, column_start, half_width, 1)
    own_part = jnp.einsum("mi,mxj->xij", my_taps, slot_lines, preferred_element_type=jnp.float32)
    far_part = jnp.einsum(
        "mi,mxj->xij", their_taps, other_lines, preferred_element_type=jnp.float32
    )
    own_round = lax.optimization_barrier(own_part.astype(jnp.bfloat16))
    far_round = lax.optimization_barrier(far_part.astype(jnp.bfloat16))
    kspace = own_round.astype(jnp.float32) + far_round.astype(jnp.float32)
    pieces_each = half_width // n_pulse
    shaped = kspace.reshape(2, n_pulse, pieces_each, band_rows)
    pieces = lax.all_to_all(
        shaped.astype(jnp.bfloat16), "pulse", split_axis=1, concat_axis=3, tiled=True
    ).astype(shaped.dtype)
    real_out, imag_out = spectral(pieces[0], pieces[1], 1.0)
    columns_done = jnp.stack([real_out, imag_out])
    columns_done = columns_done.reshape(2, pieces_each, band_rows * n_pulse)
    moved = lax.all_to_all(
        lax.all_to_all(as_sent(columns_done), "pulse", split_axis=2, concat_axis=1, tiled=True),
        ("range", "sub"),
        split_axis=2,
        concat_axis=1,
        tiled=True,
    ).astype(columns_done.dtype)
    flipped = jnp.swapaxes(moved, 1, 2)
    real_out, imag_out = spectral(flipped[0], flipped[1], 1.0)
    return jnp.stack([real_out, imag_out])


LANES = 128
BF16 = jnp.bfloat16
F32 = jnp.float32
MESH = pl.DeviceIdType.MESH


def split_bf16(table):
    high = table.astype(ml_dtypes.bfloat16)
    low = (table - high.astype(np.float64)).astype(ml_dtypes.bfloat16)
    return np.stack([high, low])


def turn(fraction):
    return np.exp(2j * np.pi * (fraction % 1.0))


def pulse_tables(samples, n_range):
    rows = samples // LANES
    k = np.arange(LANES)
    first = turn(-np.outer(k, np.arange(rows)) / rows) / math.sqrt(samples)
    parts = first.reshape(LANES, n_range, rows // n_range)
    real = np.stack([parts.real, -parts.imag], axis=2).reshape(LANES, 2 * rows)
    imag = np.stack([parts.imag, parts.real], axis=2).reshape(LANES, 2 * rows)
    left = split_bf16(np.concatenate([real, imag]))
    second = turn(-np.outer(k, k) / LANES)
    right = split_bf16(np.block([[second.real, -second.imag], [second.imag, second.real]]))
    twist = turn(-np.outer(k, k) / samples)
    return left, right, np.stack([twist.real, twist.imag]).astype(np.float32)


def column_tables(grid, n_pulse, rows, devices):
    band = grid // n_pulse
    u = np.arange(grid).reshape(n_pulse, 1, band)
    angle = turn(u * np.arange(rows)[None, :, None] / grid) / math.sqrt(grid)
    table = np.concatenate([angle.real, angle.imag], axis=2).astype(ml_dtypes.bfloat16)
    shift = turn(np.outer(np.arange(devices) * rows, np.arange(LANES)) / grid)
    return table, np.stack([shift.real, shift.imag]).astype(np.float32)[:, :, None, :]


def row_table(grid, width):
    upper = grid // LANES
    half = upper // 2
    f = np.arange(half)[:, None, None, None, None]
    e = np.arange(2)[None, :, None, None, None]
    i1 = np.arange(width // upper)[None, None, :, None, None]
    parity = np.arange(2)[None, None, None, :, None]
    x1 = np.arange(LANES)[None, None, None, None, :]
    taps = upper * i1 + half * e + f
    angle = turn(taps * x1 / grid + (half * e + f) * parity / upper) / math.sqrt(grid)
    both = np.stack([angle.real, angle.imag], axis=4)
    return both.reshape(half, 2 * (width // upper), 4 * LANES).astype(ml_dtypes.bfloat16)


def plane_transform(real, imag):
    count = len(real)
    if count == 1:
        return real, imag
    even_r, even_i = plane_transform(real[0::2], imag[0::2])
    odd_r, odd_i = plane_transform(real[1::2], imag[1::2])
    low_r, low_i, high_r, high_i = [], [], [], []
    for k in range(count // 2):
        a, b = odd_r[k], odd_i[k]
        if k == 0:
            tr, ti = a, b
        elif 4 * k == count:
            tr, ti = -b, a
        else:
            c = math.cos(2.0 * math.pi * k / count)
            s = math.sin(2.0 * math.pi * k / count)
            tr, ti = a * c - b * s, a * s + b * c
        low_r.append(even_r[k] + tr)
        low_i.append(even_i[k] + ti)
        high_r.append(even_r[k] - tr)
        high_i.append(even_i[k] - ti)
    return low_r + high_r, low_i + high_i


def matmul(a, b):
    return jnp.dot(a, b, preferred_element_type=F32)


def matmul_nt(a, b):
    return lax.dot_general(a, b, (((1,), (1,)), ((), ())), preferred_element_type=F32)


def form_kernel(
    sizes,
    raw_ref, az_ref, left_ref, right_ref, twist_ref, shift_ref, taps_ref, rowtab_ref, coltab_ref,
    lhs_ref, rhs_ref,
    x_buf, az_buf, sp_out, sp_in, sp_f32, planes, turned, col_buf, part_out, part_in, sums,
    local_sem, x_send, x_recv, az_send, az_recv, sp_send, sp_recv, part_send, part_recv,
):
    n_pulse, n_range, n_sub = sizes
    devices = n_pulse * n_range * n_sub
    z, x, s = lax.axis_index("pulse"), lax.axis_index("range"), lax.axis_index("sub")
    me = (z * n_range + x) * n_sub + s
    shards = n_pulse * n_sub
    shard = z * n_sub + s
    pulses = x_buf.shape[2]
    blocks = taps_ref.shape[0]
    band_rows = sp_in.shape[3]

    def whole_id(index):
        rest = index // n_sub
        return {"pulse": rest // n_range, "range": rest % n_range, "sub": index % n_sub}

    table_copy = pltpu.make_async_copy(coltab_ref.at[z], col_buf, local_sem.at[0])
    table_copy.start()
    own_raw = pltpu.make_async_copy(raw_ref.at[:, pl.ds(x * pulses, pulses)], x_buf.at[x], local_sem.at[1])
    own_raw.start()
    own_az = pltpu.make_async_copy(az_ref, az_buf.at[shard], local_sem.at[2])
    own_az.start()

    barrier = pltpu.get_barrier_semaphore()
    for r in range(1, devices):
        pl.semaphore_signal(barrier, inc=1, device_id=whole_id((me + r) % devices), device_id_type=MESH)
    pl.semaphore_wait(barrier, devices - 1)

    raw_copies = []
    for r in range(1, n_range):
        other = (x + r) % n_range
        copy = pltpu.make_async_remote_copy(
            raw_ref.at[:, pl.ds(other * pulses, pulses)], x_buf.at[x], x_send.at[r], x_recv.at[r],
            device_id={"pulse": z, "range": other, "sub": s}, device_id_type=MESH)
        copy.start()
        raw_copies.append(copy)
    az_copies = []
    for r in range(1, shards):
        other = (shard + r) % shards
        copy = pltpu.make_async_remote_copy(
            az_ref, az_buf.at[shard], az_send.at[r], az_recv.at[r],
            device_id={"pulse": other // n_sub, "range": x, "sub": other % n_sub}, device_id_type=MESH)
        copy.start()
        az_copies.append(copy)

    own_raw.wait()
    for copy in raw_copies:
        copy.wait()

    twist_r, twist_i = twist_ref[0], twist_ref[1]
    for p in range(pulses):
        samples = jnp.concatenate(
            [x_buf[h, c, p] for h in range(n_range) for c in range(2)], axis=0)
        mixed = matmul(left_ref[0], samples) + matmul(left_ref[1], samples)
        mr, mi = mixed[:LANES], mixed[LANES:]
        both = jnp.concatenate([mr * twist_r - mi * twist_i, mr * twist_i + mi * twist_r], axis=1)
        high = both.astype(BF16)
        low = (both - high.astype(F32)).astype(BF16)
        bins = (matmul_nt(right_ref[0], high) + matmul_nt(right_ref[1], high)
                + matmul_nt(right_ref[0], low)).astype(BF16)
        for c in range(2):
            for d in range(n_pulse):
                start = c * LANES + d * band_rows
                sp_out[d, c, p] = bins[start:start + band_rows]

    own_bins = pltpu.make_async_copy(sp_out.at[z], sp_in.at[z], local_sem.at[1])
    own_bins.start()
    bin_copies = []
    for r in range(1, n_pulse):
        other = (z + r) % n_pulse
        copy = pltpu.make_async_remote_copy(
            sp_out.at[other], sp_in.at[z], sp_send.at[r], sp_recv.at[r],
            device_id={"pulse": other, "range": x, "sub": s}, device_id_type=MESH)
        copy.start()
        bin_copies.append(copy)

    own_az.wait()
    for copy in az_copies:
        copy.wait()
    residues = rowtab_ref.shape[0]
    per_shard = az_ref.shape[0] // (residues + 2)
    everything = [az_buf[q].astype(F32) for q in range(shards)]

    def of_residue(f):
        return jnp.concatenate([a[f * per_shard:(f + 1) * per_shard] for a in everything], axis=0)

    for f in range(residues):
        planes[f] = matmul(of_residue(f).astype(BF16), rowtab_ref[f])
    total = shards * per_shard
    planes[residues, :, 0:LANES] = of_residue(residues)
    planes[residues, :, LANES:2 * LANES] = of_residue(residues + 1)
    step_rows = 16

    def row_step(i, carry):
        rows = pl.ds(pl.multiple_of(i * step_rows, step_rows), step_rows)
        rows_i = pl.ds(pl.multiple_of(total + i * step_rows, step_rows), step_rows)
        pr = planes[residues, rows, 0:LANES]
        pi = planes[residues, rows, LANES:2 * LANES]
        for parity in range(2):
            at = 2 * parity * LANES
            real = [planes[f, rows, at:at + LANES] for f in range(residues)]
            imag = [planes[f, rows, at + LANES:at + 2 * LANES] for f in range(residues)]
            real, imag = plane_transform(real, imag)
            for k in range(residues):
                lane = (2 * k + parity) * LANES
                rhs_ref[rows, lane:lane + LANES] = (real[k] * pr - imag[k] * pi).astype(BF16)
                rhs_ref[rows_i, lane:lane + LANES] = (real[k] * pi + imag[k] * pr).astype(BF16)
        return carry

    lax.fori_loop(0, total // step_rows, row_step, 0)

    own_bins.wait()
    for copy in bin_copies:
        copy.wait()
    lines = n_pulse * pulses
    for d in range(n_pulse):
        for c in range(2):
            for p in range(pulses):
                at = ((c * n_pulse + d) * pulses + p) * band_rows
                sp_f32[at:at + band_rows] = sp_in[d, c, p].astype(F32)
    per_block = band_rows // blocks
    band = blocks * LANES
    shift_r, shift_i = shift_ref[0], shift_ref[1]
    for b in range(blocks):
        bins = jnp.concatenate(
            [sp_f32[pl.ds(b * per_block + q, 2 * lines, stride=band_rows), :] for q in range(per_block)], axis=1)
        line = matmul(bins.astype(BF16), taps_ref[b]).astype(BF16).astype(F32)
        kr, ki = line[None, :lines], line[None, lines:]
        tr = (kr * shift_r - ki * shift_i).astype(BF16)
        ti = (kr * shift_i + ki * shift_r).astype(BF16)
        lane = b * LANES
        turned[:, 0:lines, lane:lane + LANES] = tr
        turned[:, 0:lines, band + lane:band + lane + LANES] = -ti
        turned[:, lines:2 * lines, lane:lane + LANES] = ti
        turned[:, lines:2 * lines, band + lane:band + lane + LANES] = tr
    table_copy.wait()
    part = matmul_nt(turned[...].reshape(devices * 2 * lines, 2 * band), col_buf[...])
    part_out[...] = part.astype(BF16).reshape(part_out.shape)

    own_part = pltpu.make_async_copy(part_out.at[me], part_in.at[me], local_sem.at[1])
    own_part.start()
    part_copies = []
    for r in range(1, devices):
        other = (me + r) % devices
        copy = pltpu.make_async_remote_copy(
            part_out.at[other], part_in.at[me], part_send.at[r], part_recv.at[r],
            device_id=whole_id(other), device_id_type=MESH)
        copy.start()
        part_copies.append(copy)
    own_part.wait()
    for copy in part_copies:
        copy.wait()

    per_sub = n_range * n_sub
    out_rows = col_buf.shape[0]
    for k in range(per_sub):
        acc = part_in[k].astype(F32)
        for d in range(1, n_pulse):
            acc = acc + part_in[d * per_sub + k].astype(F32)
        xx, ss = k // n_sub, k % n_sub
        for c in range(2):
            for d in range(n_pulse):
                src = c * lines + d * pulses
                dst = c * total + ((d * n_sub + ss) * n_range + xx) * pulses
                sums[dst:dst + pulses, :] = acc[src:src + pulses]
    real = jnp.transpose(sums[0:total, :])
    imag = jnp.transpose(sums[total:2 * total, :])
    lhs_ref[0:out_rows, :] = jnp.concatenate([real, -imag], axis=1).astype(BF16)
    lhs_ref[out_rows:2 * out_rows, :] = jnp.concatenate([imag, real], axis=1).astype(BF16)


def low_rank_body(raw_echo, range_taps, azim_taps, tile_col):
    n_range, n_pulse, n_sub = lax.axis_size("range"), lax.axis_size("pulse"), lax.axis_size("sub")
    devices = n_range * n_pulse * n_sub
    shard_pulses, shard_samples = raw_echo.shape[1], raw_echo.shape[2]
    samples = shard_samples * n_range
    pulses = shard_pulses // n_range
    blocks, block_bins, block_rows = range_taps.shape
    grid = blocks * block_rows * n_pulse
    width = azim_taps.shape[1]
    tiles = grid // width
    rows = grid // devices
    upper = grid // LANES
    half = upper // 2
    total = shard_pulses * n_pulse * n_sub
    lines = n_pulse * pulses
    band_rows = samples // LANES // n_pulse

    raw = raw_echo.reshape(2, shard_pulses, shard_samples // LANES, LANES)
    az = azim_taps.reshape(shard_pulses, width // upper, 2, half).transpose(3, 0, 2, 1)
    az = az.reshape(half, shard_pulses, LANES)
    phase = (tile_col * jnp.arange(LANES, dtype=jnp.int32)[None, :] % tiles).astype(F32) * (2.0 * math.pi / tiles)
    az = jnp.concatenate([az, jnp.stack([jnp.cos(phase), jnp.sin(phase)]).astype(BF16)])
    az = az.reshape((half + 2) * shard_pulses, LANES)
    left, right, twist = pulse_tables(samples, n_range)
    coltab, shift = column_tables(grid, n_pulse, rows, devices)
    rowtab = row_table(grid, width)

    vmem = pl.BlockSpec(memory_space=pltpu.VMEM)
    lhs, rhs = pl.pallas_call(
        functools.partial(form_kernel, (n_pulse, n_range, n_sub)),
        out_shape=(
            jax.ShapeDtypeStruct((2 * rows, 2 * total), BF16),
            jax.ShapeDtypeStruct((2 * total, grid), BF16),
        ),
        in_specs=[vmem] * 8 + [pl.BlockSpec(memory_space=pl.ANY)],
        out_specs=(vmem, vmem),
        scratch_shapes=[
            pltpu.VMEM((n_range, 2, pulses, shard_samples // LANES, LANES), BF16),
            pltpu.VMEM((n_pulse * n_sub,) + az.shape, BF16),
            pltpu.VMEM((n_pulse, 2, pulses, band_rows, LANES), BF16),
            pltpu.VMEM((n_pulse, 2, pulses, band_rows, LANES), BF16),
            pltpu.VMEM((2 * lines * band_rows, LANES), F32),
            pltpu.VMEM((half + 1, total, 4 * LANES), F32),
            pltpu.VMEM((devices, 2 * lines, 2 * grid // n_pulse), BF16),
            pltpu.VMEM((rows, 2 * grid // n_pulse), BF16),
            pltpu.VMEM((devices, 2 * lines, rows), BF16),
            pltpu.VMEM((devices, 2 * lines, rows), BF16),
            pltpu.VMEM((2 * total, rows), F32),
            pltpu.SemaphoreType.DMA((3,)),
            pltpu.SemaphoreType.DMA((n_range,)),
            pltpu.SemaphoreType.DMA((n_range,)),
            pltpu.SemaphoreType.DMA((n_pulse * n_sub,)),
            pltpu.SemaphoreType.DMA((n_pulse * n_sub,)),
            pltpu.SemaphoreType.DMA((n_pulse,)),
            pltpu.SemaphoreType.DMA((n_pulse,)),
            pltpu.SemaphoreType.DMA((devices,)),
            pltpu.SemaphoreType.DMA((devices,)),
        ],
        compiler_params=pltpu.CompilerParams(
            collective_id=0, has_side_effects=True, vmem_limit_bytes=40 * 2 ** 20),
    )(raw, az, left, right, twist, shift, range_taps, rowtab, coltab)
    image = jnp.dot(lhs, rhs, preferred_element_type=F32)
    return image.reshape(2, rows, grid)


def body(raw_echo, range_taps, azim_taps, tile_col):
    n_range, n_pulse, n_sub = lax.axis_size("range"), lax.axis_size("pulse"), lax.axis_size("sub")
    samples = raw_echo.shape[2] * n_range
    grid = range_taps.shape[0] * range_taps.shape[2] * n_pulse
    pulses = raw_echo.shape[1] * n_pulse * n_sub
    band_rows = samples // LANES // n_pulse
    low_rank = 16 * pulses <= grid
    fits = (
        samples == LANES * LANES
        and azim_taps.shape[1] * 2 * LANES == grid * LANES
        and grid // LANES * LANES == grid
        and azim_taps.shape[1] // (grid // LANES) * 2 == LANES
        and range_taps.shape[2] == LANES
        and band_rows % 16 == 0
        and pulses % 16 == 0
        and raw_echo.shape[1] == 8
        and grid // (n_range * n_pulse * n_sub) % LANES == 0
    )
    if low_rank and fits:
        return low_rank_body(raw_echo, range_taps, azim_taps, tile_col)
    return general_body(raw_echo, range_taps, azim_taps, tile_col)


def solution(mesh):
    placed = (
        P(None, ("groups", "pulse", "sub"), "range"),
        P("pulse", None, None),
        P(("groups", "pulse", "sub"), None),
        P(("groups", "pulse", "sub"), None),
    )
    return jax.shard_map(
        body,
        mesh=mesh,
        in_specs=placed,
        out_specs=P(None, ("groups", "pulse", "range", "sub"), None),
        check_vma=False,
    )
```

```python
import functools
import math

import jax
import jax.numpy as jnp
import ml_dtypes
import numpy as np
from jax import lax
from jax.experimental import pallas as pl
from jax.experimental.pallas import tpu as pltpu
from jax.sharding import PartitionSpec as P

CAP = 2


def swapped(block, axis, bit):
    count = lax.axis_size(axis)
    route = []
    for low in range(count):
        high = low | 1 << bit
        if high != low and high < count:
            route += [(low, high), (high, low)]
    return lax.ppermute(block, axis, route)


def as_sent(value):
    return jax.tree.map(lambda a: a.astype(jnp.bfloat16) if a.dtype == jnp.float32 else a, value)


def tables(points, direction):
    indices = jnp.arange(points, dtype=jnp.int32)
    phases = indices[:, None] * indices[None, :] % points
    angles = phases.astype(jnp.float32) * (2.0 * math.pi / points)
    return (jnp.cos(angles), direction * jnp.sin(angles))


def spectral(real_part, imag_part, direction):
    length = real_part.shape[-1]
    outer_len = 1 << (length.bit_length() - 1) // 2
    inner_len = length // outer_len
    leading = real_part.shape[:-1]
    real_part = real_part.reshape(leading + (outer_len, inner_len))
    imag_part = imag_part.reshape(leading + (outer_len, inner_len))
    highest = lax.Precision.HIGHEST
    cos_outer, sin_outer = tables(outer_len, direction)
    mixed_real = jnp.einsum(
        "...nm,nk->...km", real_part, cos_outer, precision=highest
    ) - jnp.einsum("...nm,nk->...km", imag_part, sin_outer, precision=highest)
    mixed_imag = jnp.einsum(
        "...nm,nk->...km", real_part, sin_outer, precision=highest
    ) + jnp.einsum("...nm,nk->...km", imag_part, cos_outer, precision=highest)
    outer_index = jnp.arange(outer_len, dtype=jnp.int32)[:, None]
    inner_index = jnp.arange(inner_len, dtype=jnp.int32)[None, :]
    twists = (outer_index * inner_index % length).astype(jnp.float32) * (2.0 * math.pi / length)
    twist_cos = jnp.cos(twists)
    twist_sin = direction * jnp.sin(twists)
    turned_real = mixed_real * twist_cos - mixed_imag * twist_sin
    turned_imag = mixed_real * twist_sin + mixed_imag * twist_cos
    cos_inner, sin_inner = tables(inner_len, direction)
    final_real = jnp.einsum(
        "...km,mj->...jk", turned_real, cos_inner, precision=highest
    ) - jnp.einsum("...km,mj->...jk", turned_imag, sin_inner, precision=highest)
    final_imag = jnp.einsum(
        "...km,mj->...jk", turned_real, sin_inner, precision=highest
    ) + jnp.einsum("...km,mj->...jk", turned_imag, cos_inner, precision=highest)
    norm_scale = 1.0 / math.sqrt(length)
    return (
        (final_real * norm_scale).reshape(leading + (length,)),
        (final_imag * norm_scale).reshape(leading + (length,)),
    )


def general_body(raw_echo, range_taps, azim_taps, tile_col):
    n_range = lax.axis_size("range")
    n_pulse = lax.axis_size("pulse")
    my_range = lax.axis_index("range")
    my_sub = lax.axis_index("sub")
    shard_pulses = raw_echo.shape[1]
    shard_samples = raw_echo.shape[2]
    per_device = shard_pulses // n_range
    grouped = raw_echo.reshape(2, n_range, per_device, shard_samples)
    pieces = lax.all_to_all(grouped, "range", split_axis=1, concat_axis=3, tiled=True)
    real_out, imag_out = spectral(
        pieces[0].astype(jnp.float32), pieces[1].astype(jnp.float32), -1.0
    )
    spectrum = jnp.stack([real_out, imag_out]).astype(jnp.bfloat16)
    spectrum = spectrum.reshape(2, per_device, shard_samples * n_range)
    band_bins = spectrum.shape[2] // n_pulse
    first_pulse = my_range * per_device
    cols_here = lax.dynamic_slice_in_dim(tile_col[:, 0], first_pulse, per_device)
    taps_here = lax.dynamic_slice_in_dim(azim_taps, first_pulse, per_device, 0)
    position = jnp.arange(per_device, dtype=jnp.int32)
    earlier = position[None, :] < position[:, None]
    same_tile = cols_here[:, None] == cols_here[None, :]
    slot_rank = jnp.sum(jnp.where(earlier & same_tile, 1, 0), axis=1)
    tile_ids = jnp.arange(n_range, dtype=jnp.int32)
    slot_ids = jnp.arange(CAP, dtype=jnp.int32)
    placing = (
        (cols_here[None, None, :] == tile_ids[:, None, None])
        & (slot_rank[None, None, :] == slot_ids[None, :, None])
    ).astype(jnp.bfloat16)
    banded = spectrum.reshape(2, per_device, n_pulse, band_bins)
    send_lines = jnp.einsum(
        "tcq,xqpb->ptcxb", placing, banded, preferred_element_type=jnp.float32
    ).astype(jnp.bfloat16)
    send_taps = jnp.einsum(
        "tcq,qw->tcw", placing, taps_here, preferred_element_type=jnp.float32
    ).astype(jnp.bfloat16)
    tile_width = send_taps.shape[2]
    send_taps = jnp.broadcast_to(send_taps[None], (n_pulse, n_range, CAP, tile_width))
    block_count, block_bins, block_rows = range_taps.shape
    flat_lines = send_lines.reshape(n_pulse * n_range, CAP, 2, band_bins)
    flat_taps = send_taps.reshape(n_pulse * n_range, CAP, tile_width)
    line_block = lax.all_to_all(
        flat_lines, ("pulse", "range"), split_axis=0, concat_axis=0, tiled=True
    )
    tap_block = lax.all_to_all(
        flat_taps, ("pulse", "range"), split_axis=0, concat_axis=0, tiled=True
    )
    blocked = line_block.reshape(line_block.shape[:3] + (block_count, block_bins))
    resampled = jnp.einsum(
        "skxbr,brj->skxbj", blocked, range_taps, preferred_element_type=jnp.float32
    )
    ky_rows = resampled.reshape(line_block.shape[:3] + (block_count * block_rows,)).astype(
        jnp.bfloat16
    )
    band_rows = ky_rows.shape[3]
    slot_total = ky_rows.shape[0] * ky_rows.shape[1]
    slot_lines = ky_rows.reshape(slot_total, 2, band_rows)
    slot_taps = tap_block.reshape(slot_total, tile_width)
    half_width = tile_width // 2
    other_lines, other_taps = swapped((slot_lines, slot_taps), "sub", 0)
    column_start = my_sub * half_width
    my_taps = lax.dynamic_slice_in_dim(slot_taps, column_start, half_width, 1)
    their_taps = lax.dynamic_slice_in_dim(other_taps, column_start, half_width, 1)
    own_part = jnp.einsum("mi,mxj->xij", my_taps, slot_lines, preferred_element_type=jnp.float32)
    far_part = jnp.einsum(
        "mi,mxj->xij", their_taps, other_lines, preferred_element_type=jnp.float32
    )
    own_round = lax.optimization_barrier(own_part.astype(jnp.bfloat16))
    far_round = lax.optimization_barrier(far_part.astype(jnp.bfloat16))
    kspace = own_round.astype(jnp.float32) + far_round.astype(jnp.float32)
    pieces_each = half_width // n_pulse
    shaped = kspace.reshape(2, n_pulse, pieces_each, band_rows)
    pieces = lax.all_to_all(
        shaped.astype(jnp.bfloat16), "pulse", split_axis=1, concat_axis=3, tiled=True
    ).astype(shaped.dtype)
    real_out, imag_out = spectral(pieces[0], pieces[1], 1.0)
    columns_done = jnp.stack([real_out, imag_out])
    columns_done = columns_done.reshape(2, pieces_each, band_rows * n_pulse)
    moved = lax.all_to_all(
        lax.all_to_all(as_sent(columns_done), "pulse", split_axis=2, concat_axis=1, tiled=True),
        ("range", "sub"),
        split_axis=2,
        concat_axis=1,
        tiled=True,
    ).astype(columns_done.dtype)
    flipped = jnp.swapaxes(moved, 1, 2)
    real_out, imag_out = spectral(flipped[0], flipped[1], 1.0)
    return jnp.stack([real_out, imag_out])


LANES = 128
BF16 = jnp.bfloat16
F32 = jnp.float32
MESH = pl.DeviceIdType.MESH


def split_bf16(table):
    high = table.astype(ml_dtypes.bfloat16)
    low = (table - high.astype(np.float64)).astype(ml_dtypes.bfloat16)
    return np.stack([high, low])


def turn(fraction):
    return np.exp(2j * np.pi * (fraction % 1.0))


def pulse_tables(samples, n_range):
    rows = samples // LANES
    k = np.arange(LANES)
    first = turn(-np.outer(k, np.arange(rows)) / rows) / math.sqrt(samples)
    parts = first.reshape(LANES, n_range, rows // n_range)
    real = np.stack([parts.real, -parts.imag], axis=2).reshape(LANES, 2 * rows)
    imag = np.stack([parts.imag, parts.real], axis=2).reshape(LANES, 2 * rows)
    left = split_bf16(np.concatenate([real, imag]))
    second = turn(-np.outer(k, k) / LANES)
    right = split_bf16(np.block([[second.real, -second.imag], [second.imag, second.real]]))
    twist = turn(-np.outer(k, k) / samples)
    return left, right, np.stack([twist.real, twist.imag]).astype(np.float32)


def column_tables(grid, n_pulse, rows, devices):
    band = grid // n_pulse
    u = np.arange(grid).reshape(n_pulse, 1, band)
    angle = turn(u * np.arange(rows)[None, :, None] / grid) / math.sqrt(grid)
    table = np.concatenate([angle.real, angle.imag], axis=2).astype(ml_dtypes.bfloat16)
    shift = turn(np.outer(np.arange(devices) * rows, np.arange(LANES)) / grid)
    return table, np.stack([shift.real, shift.imag]).astype(np.float32)[:, :, None, :]


def row_table(grid, width):
    upper = grid // LANES
    half = upper // 2
    f = np.arange(half)[:, None, None, None, None]
    e = np.arange(2)[None, :, None, None, None]
    i1 = np.arange(width // upper)[None, None, :, None, None]
    parity = np.arange(2)[None, None, None, :, None]
    x1 = np.arange(LANES)[None, None, None, None, :]
    taps = upper * i1 + half * e + f
    angle = turn(taps * x1 / grid + (half * e + f) * parity / upper) / math.sqrt(grid)
    both = np.stack([angle.real, angle.imag], axis=4)
    return both.reshape(half, 2 * (width // upper), 4 * LANES).astype(ml_dtypes.bfloat16)


def plane_transform(real, imag):
    count = len(real)
    if count == 1:
        return real, imag
    even_r, even_i = plane_transform(real[0::2], imag[0::2])
    odd_r, odd_i = plane_transform(real[1::2], imag[1::2])
    low_r, low_i, high_r, high_i = [], [], [], []
    for k in range(count // 2):
        a, b = odd_r[k], odd_i[k]
        if k == 0:
            tr, ti = a, b
        elif 4 * k == count:
            tr, ti = -b, a
        else:
            c = math.cos(2.0 * math.pi * k / count)
            s = math.sin(2.0 * math.pi * k / count)
            tr, ti = a * c - b * s, a * s + b * c
        low_r.append(even_r[k] + tr)
        low_i.append(even_i[k] + ti)
        high_r.append(even_r[k] - tr)
        high_i.append(even_i[k] - ti)
    return low_r + high_r, low_i + high_i


def matmul(a, b):
    return jnp.dot(a, b, preferred_element_type=F32)


def matmul_nt(a, b):
    return lax.dot_general(a, b, (((1,), (1,)), ((), ())), preferred_element_type=F32)


def form_kernel(
    sizes,
    raw_ref, az_ref, left_hbm, right_hbm, twist_hbm, shift_hbm, taps_hbm, rowtab_hbm, coltab_hbm,
    lhs_ref, rhs_ref,
    left_ref, right_ref, twist_ref, shift_ref, taps_ref, rowtab_ref, x_buf, az_buf, sp_out, sp_in, sp_f32, planes, turned, col_buf, part_out, part_in, sums,
    table_sem, local_sem, x_send, x_recv, az_send, az_recv, sp_send, sp_recv, part_send, part_recv,
):
    n_pulse, n_range, n_sub = sizes
    devices = n_pulse * n_range * n_sub
    z, x, s = lax.axis_index("pulse"), lax.axis_index("range"), lax.axis_index("sub")
    me = (z * n_range + x) * n_sub + s
    shards = n_pulse * n_sub
    shard = z * n_sub + s
    pulses = x_buf.shape[2]
    blocks = taps_hbm.shape[0]
    band_rows = sp_in.shape[3]

    def whole_id(index):
        rest = index // n_sub
        return {"pulse": rest // n_range, "range": rest % n_range, "sub": index % n_sub}

    tables = [
        pltpu.make_async_copy(source, target, table_sem.at[i])
        for i, (source, target) in enumerate([
            (left_hbm, left_ref), (twist_hbm, twist_ref), (right_hbm, right_ref), (rowtab_hbm, rowtab_ref),
            (taps_hbm, taps_ref), (shift_hbm, shift_ref), (coltab_hbm.at[z], col_buf)])]
    left_copy, twist_copy, right_copy, row_copy, taps_copy, shift_copy, table_copy = tables
    for copy in tables:
        copy.start()
    own_raw = pltpu.make_async_copy(raw_ref.at[:, pl.ds(x * pulses, pulses)], x_buf.at[x], local_sem.at[1])
    own_raw.start()
    own_az = pltpu.make_async_copy(az_ref, az_buf.at[shard], local_sem.at[2])
    own_az.start()

    barrier = pltpu.get_barrier_semaphore()
    for r in range(1, devices):
        pl.semaphore_signal(barrier, inc=1, device_id=whole_id((me + r) % devices), device_id_type=MESH)
    pl.semaphore_wait(barrier, devices - 1)

    raw_copies = []
    for r in range(1, n_range):
        other = (x + r) % n_range
        copy = pltpu.make_async_remote_copy(
            raw_ref.at[:, pl.ds(other * pulses, pulses)], x_buf.at[x], x_send.at[r], x_recv.at[r],
            device_id={"pulse": z, "range": other, "sub": s}, device_id_type=MESH)
        copy.start()
        raw_copies.append(copy)
    az_copies = []
    for r in range(1, shards):
        other = (shard + r) % shards
        copy = pltpu.make_async_remote_copy(
            az_ref, az_buf.at[shard], az_send.at[r], az_recv.at[r],
            device_id={"pulse": other // n_sub, "range": x, "sub": other % n_sub}, device_id_type=MESH)
        copy.start()
        az_copies.append(copy)

    own_raw.wait()
    for copy in raw_copies:
        copy.wait()

    left_copy.wait()
    twist_copy.wait()
    right_copy.wait()
    twist_r, twist_i = twist_ref[0], twist_ref[1]
    samples = jnp.concatenate(
        [jnp.concatenate([x_buf[h, c, p] for h in range(n_range) for c in range(2)], axis=0)
         for p in range(pulses)], axis=1)
    mixed = matmul(left_ref[0], samples) + matmul(left_ref[1], samples)
    both = []
    for p in range(pulses):
        lanes = slice(p * LANES, (p + 1) * LANES)
        mr, mi = mixed[:LANES, lanes], mixed[LANES:, lanes]
        both.append(jnp.concatenate([mr * twist_r - mi * twist_i, mr * twist_i + mi * twist_r], axis=1))
    both = jnp.concatenate(both, axis=0)
    high = both.astype(BF16)
    low = (both - high.astype(F32)).astype(BF16)
    bins = (matmul_nt(right_ref[0], high) + matmul_nt(right_ref[1], high)
            + matmul_nt(right_ref[0], low)).astype(BF16)
    for c in range(2):
        for d in range(n_pulse):
            for p in range(pulses):
                start = c * LANES + d * band_rows
                sp_out[d, c, p] = bins[start:start + band_rows, p * LANES:(p + 1) * LANES]
    own_bins = pltpu.make_async_copy(sp_out.at[z], sp_in.at[z], local_sem.at[1])
    own_bins.start()
    bin_copies = []
    for r in range(1, n_pulse):
        other = (z + r) % n_pulse
        copy = pltpu.make_async_remote_copy(
            sp_out.at[other], sp_in.at[z], sp_send.at[r], sp_recv.at[r],
            device_id={"pulse": other, "range": x, "sub": s}, device_id_type=MESH)
        copy.start()
        bin_copies.append(copy)

    own_az.wait()
    for copy in az_copies:
        copy.wait()
    row_copy.wait()
    residues = rowtab_ref.shape[0]
    per_shard = az_ref.shape[0] // (residues + 2)
    total = shards * per_shard
    everything = [az_buf[q].astype(F32) for q in range(shards)]

    def of_residue(f):
        return jnp.concatenate([a[f * per_shard:(f + 1) * per_shard] for a in everything], axis=0)

    for f in range(residues):
        planes[f] = matmul(of_residue(f).astype(BF16), rowtab_ref[f])
    planes[residues, :, 0:LANES] = of_residue(residues)
    planes[residues, :, LANES:2 * LANES] = of_residue(residues + 1)
    own_bins.wait()
    for copy in bin_copies:
        copy.wait()
    lines = n_pulse * pulses
    taps_copy.wait()
    shift_copy.wait()
    table_copy.wait()
    for d in range(n_pulse):
        for c in range(2):
            for p in range(pulses):
                at = ((c * n_pulse + d) * pulses + p) * band_rows
                sp_f32[at:at + band_rows] = sp_in[d, c, p].astype(F32)
    per_block = band_rows // blocks
    band = blocks * LANES
    shift_r, shift_i = shift_ref[0], shift_ref[1]
    for b in range(blocks):
        bins = jnp.concatenate(
            [sp_f32[pl.ds(b * per_block + q, 2 * lines, stride=band_rows), :] for q in range(per_block)], axis=1)
        line = matmul(bins.astype(BF16), taps_ref[b]).astype(BF16).astype(F32)
        kr, ki = line[None, :lines], line[None, lines:]
        tr = (kr * shift_r - ki * shift_i).astype(BF16)
        ti = (kr * shift_i + ki * shift_r).astype(BF16)
        lane = b * LANES
        turned[:, 0:lines, lane:lane + LANES] = tr
        turned[:, 0:lines, band + lane:band + lane + LANES] = -ti
        turned[:, lines:2 * lines, lane:lane + LANES] = ti
        turned[:, lines:2 * lines, band + lane:band + lane + LANES] = tr
    part = matmul_nt(turned[...].reshape(devices * 2 * lines, 2 * band), col_buf[...])
    part_out[...] = part.astype(BF16).reshape(part_out.shape)

    own_part = pltpu.make_async_copy(part_out.at[me], part_in.at[me], local_sem.at[1])
    own_part.start()
    part_copies = []
    for r in range(1, devices):
        other = (me + r) % devices
        copy = pltpu.make_async_remote_copy(
            part_out.at[other], part_in.at[me], part_send.at[r], part_recv.at[r],
            device_id=whole_id(other), device_id_type=MESH)
        copy.start()
        part_copies.append(copy)
    step_rows = 16

    def row_step(i, carry):
        rows = pl.ds(pl.multiple_of(i * step_rows, step_rows), step_rows)
        rows_i = pl.ds(pl.multiple_of(total + i * step_rows, step_rows), step_rows)
        pr = planes[residues, rows, 0:LANES]
        pi = planes[residues, rows, LANES:2 * LANES]
        for parity in range(2):
            at = 2 * parity * LANES
            real = [planes[f, rows, at:at + LANES] for f in range(residues)]
            imag = [planes[f, rows, at + LANES:at + 2 * LANES] for f in range(residues)]
            real, imag = plane_transform(real, imag)
            for k in range(residues):
                lane = (2 * k + parity) * LANES
                rhs_ref[rows, lane:lane + LANES] = (real[k] * pr - imag[k] * pi).astype(BF16)
                rhs_ref[rows_i, lane:lane + LANES] = (real[k] * pi + imag[k] * pr).astype(BF16)
        return carry

    lax.fori_loop(0, total // step_rows, row_step, 0)

    own_part.wait()
    for copy in part_copies:
        copy.wait()

    per_sub = n_range * n_sub
    out_rows = col_buf.shape[0]
    for k in range(per_sub):
        acc = part_in[k].astype(F32)
        for d in range(1, n_pulse):
            acc = acc + part_in[d * per_sub + k].astype(F32)
        xx, ss = k // n_sub, k % n_sub
        for c in range(2):
            for d in range(n_pulse):
                src = c * lines + d * pulses
                dst = c * total + ((d * n_sub + ss) * n_range + xx) * pulses
                sums[dst:dst + pulses, :] = acc[src:src + pulses]
    real = jnp.transpose(sums[0:total, :])
    imag = jnp.transpose(sums[total:2 * total, :])
    lhs_ref[0:out_rows, :] = jnp.concatenate([real, -imag], axis=1).astype(BF16)
    lhs_ref[out_rows:2 * out_rows, :] = jnp.concatenate([imag, real], axis=1).astype(BF16)


def low_rank_body(raw_echo, range_taps, azim_taps, tile_col):
    n_range, n_pulse, n_sub = lax.axis_size("range"), lax.axis_size("pulse"), lax.axis_size("sub")
    devices = n_range * n_pulse * n_sub
    shard_pulses, shard_samples = raw_echo.shape[1], raw_echo.shape[2]
    samples = shard_samples * n_range
    pulses = shard_pulses // n_range
    blocks, block_bins, block_rows = range_taps.shape
    grid = blocks * block_rows * n_pulse
    width = azim_taps.shape[1]
    tiles = grid // width
    rows = grid // devices
    upper = grid // LANES
    half = upper // 2
    total = shard_pulses * n_pulse * n_sub
    lines = n_pulse * pulses
    band_rows = samples // LANES // n_pulse

    raw = raw_echo.reshape(2, shard_pulses, shard_samples // LANES, LANES)
    az = azim_taps.reshape(shard_pulses, width // upper, 2, half).transpose(3, 0, 2, 1)
    az = az.reshape(half, shard_pulses, LANES)
    offsets = turn(np.outer(np.arange(tiles), np.arange(LANES)) / tiles)
    offsets = np.stack([offsets.real, offsets.imag]).astype(np.float32)
    phase = sum(jnp.where(tile_col[None] == t, offsets[:, None, t], 0.0) for t in range(tiles))
    az = jnp.concatenate([az, phase.astype(BF16)])
    az = az.reshape((half + 2) * shard_pulses, LANES)
    left, right, twist = pulse_tables(samples, n_range)
    coltab, shift = column_tables(grid, n_pulse, rows, devices)
    rowtab = row_table(grid, width)

    vmem = pl.BlockSpec(memory_space=pltpu.VMEM)
    lhs, rhs = pl.pallas_call(
        functools.partial(form_kernel, (n_pulse, n_range, n_sub)),
        out_shape=(
            jax.ShapeDtypeStruct((2 * rows, 2 * total), BF16),
            jax.ShapeDtypeStruct((2 * total, grid), BF16),
        ),
        in_specs=[vmem] * 2 + [pl.BlockSpec(memory_space=pltpu.HBM)] * 7,
        out_specs=(vmem, vmem),
        scratch_shapes=[
            pltpu.VMEM(left.shape, BF16),
            pltpu.VMEM(right.shape, BF16),
            pltpu.VMEM(twist.shape, F32),
            pltpu.VMEM(shift.shape, F32),
            pltpu.VMEM(range_taps.shape, BF16),
            pltpu.VMEM(rowtab.shape, BF16),
            pltpu.VMEM((n_range, 2, pulses, shard_samples // LANES, LANES), BF16),
            pltpu.VMEM((n_pulse * n_sub,) + az.shape, BF16),
            pltpu.VMEM((n_pulse, 2, pulses, band_rows, LANES), BF16),
            pltpu.VMEM((n_pulse, 2, pulses, band_rows, LANES), BF16),
            pltpu.VMEM((2 * lines * band_rows, LANES), F32),
            pltpu.VMEM((half + 1, total, 4 * LANES), F32),
            pltpu.VMEM((devices, 2 * lines, 2 * grid // n_pulse), BF16),
            pltpu.VMEM((rows, 2 * grid // n_pulse), BF16),
            pltpu.VMEM((devices, 2 * lines, rows), BF16),
            pltpu.VMEM((devices, 2 * lines, rows), BF16),
            pltpu.VMEM((2 * total, rows), F32),
            pltpu.SemaphoreType.DMA((7,)),
            pltpu.SemaphoreType.DMA((3,)),
            pltpu.SemaphoreType.DMA((n_range,)),
            pltpu.SemaphoreType.DMA((n_range,)),
            pltpu.SemaphoreType.DMA((n_pulse * n_sub,)),
            pltpu.SemaphoreType.DMA((n_pulse * n_sub,)),
            pltpu.SemaphoreType.DMA((n_pulse,)),
            pltpu.SemaphoreType.DMA((n_pulse,)),
            pltpu.SemaphoreType.DMA((devices,)),
            pltpu.SemaphoreType.DMA((devices,)),
        ],
        compiler_params=pltpu.CompilerParams(
            collective_id=0, has_side_effects=True, vmem_limit_bytes=60 * 2 ** 20),
    )(raw, az, left, right, twist, shift, range_taps, rowtab, coltab)
    image = jnp.dot(lhs, rhs, preferred_element_type=F32)
    return image.reshape(2, rows, grid)


def body(raw_echo, range_taps, azim_taps, tile_col):
    n_range, n_pulse, n_sub = lax.axis_size("range"), lax.axis_size("pulse"), lax.axis_size("sub")
    samples = raw_echo.shape[2] * n_range
    grid = range_taps.shape[0] * range_taps.shape[2] * n_pulse
    pulses = raw_echo.shape[1] * n_pulse * n_sub
    band_rows = samples // LANES // n_pulse
    low_rank = 16 * pulses <= grid
    fits = (
        samples == LANES * LANES
        and grid // LANES * LANES == grid
        and azim_taps.shape[1] // (grid // LANES) * 2 == LANES
        and range_taps.shape[2] == LANES
        and band_rows % 16 == 0
        and pulses % 16 == 0
        and raw_echo.shape[1] == 8
        and grid // (n_range * n_pulse * n_sub) % LANES == 0
    )
    if low_rank and fits:
        return low_rank_body(raw_echo, range_taps, azim_taps, tile_col)
    return general_body(raw_echo, range_taps, azim_taps, tile_col)


def solution(mesh):
    placed = (
        P(None, ("groups", "pulse", "sub"), "range"),
        P("pulse", None, None),
        P(("groups", "pulse", "sub"), None),
        P(("groups", "pulse", "sub"), None),
    )
    return jax.shard_map(
        body,
        mesh=mesh,
        in_specs=placed,
        out_specs=P(None, ("groups", "pulse", "range", "sub"), None),
        check_vma=False,
    )
```

```python
import functools
import math

import jax
import jax.numpy as jnp
import ml_dtypes
import numpy as np
from jax import lax
from jax.experimental import pallas as pl
from jax.experimental.pallas import tpu as pltpu
from jax.sharding import PartitionSpec as P

CAP = 2


def swapped(block, axis, bit):
    count = lax.axis_size(axis)
    route = []
    for low in range(count):
        high = low | 1 << bit
        if high != low and high < count:
            route += [(low, high), (high, low)]
    return lax.ppermute(block, axis, route)


def as_sent(value):
    return jax.tree.map(lambda a: a.astype(jnp.bfloat16) if a.dtype == jnp.float32 else a, value)


def tables(points, direction):
    indices = jnp.arange(points, dtype=jnp.int32)
    phases = indices[:, None] * indices[None, :] % points
    angles = phases.astype(jnp.float32) * (2.0 * math.pi / points)
    return (jnp.cos(angles), direction * jnp.sin(angles))


def spectral(real_part, imag_part, direction):
    length = real_part.shape[-1]
    outer_len = 1 << (length.bit_length() - 1) // 2
    inner_len = length // outer_len
    leading = real_part.shape[:-1]
    real_part = real_part.reshape(leading + (outer_len, inner_len))
    imag_part = imag_part.reshape(leading + (outer_len, inner_len))
    highest = lax.Precision.HIGHEST
    cos_outer, sin_outer = tables(outer_len, direction)
    mixed_real = jnp.einsum(
        "...nm,nk->...km", real_part, cos_outer, precision=highest
    ) - jnp.einsum("...nm,nk->...km", imag_part, sin_outer, precision=highest)
    mixed_imag = jnp.einsum(
        "...nm,nk->...km", real_part, sin_outer, precision=highest
    ) + jnp.einsum("...nm,nk->...km", imag_part, cos_outer, precision=highest)
    outer_index = jnp.arange(outer_len, dtype=jnp.int32)[:, None]
    inner_index = jnp.arange(inner_len, dtype=jnp.int32)[None, :]
    twists = (outer_index * inner_index % length).astype(jnp.float32) * (2.0 * math.pi / length)
    twist_cos = jnp.cos(twists)
    twist_sin = direction * jnp.sin(twists)
    turned_real = mixed_real * twist_cos - mixed_imag * twist_sin
    turned_imag = mixed_real * twist_sin + mixed_imag * twist_cos
    cos_inner, sin_inner = tables(inner_len, direction)
    final_real = jnp.einsum(
        "...km,mj->...jk", turned_real, cos_inner, precision=highest
    ) - jnp.einsum("...km,mj->...jk", turned_imag, sin_inner, precision=highest)
    final_imag = jnp.einsum(
        "...km,mj->...jk", turned_real, sin_inner, precision=highest
    ) + jnp.einsum("...km,mj->...jk", turned_imag, cos_inner, precision=highest)
    norm_scale = 1.0 / math.sqrt(length)
    return (
        (final_real * norm_scale).reshape(leading + (length,)),
        (final_imag * norm_scale).reshape(leading + (length,)),
    )


def general_body(raw_echo, range_taps, azim_taps, tile_col):
    n_range = lax.axis_size("range")
    n_pulse = lax.axis_size("pulse")
    my_range = lax.axis_index("range")
    my_sub = lax.axis_index("sub")
    shard_pulses = raw_echo.shape[1]
    shard_samples = raw_echo.shape[2]
    per_device = shard_pulses // n_range
    grouped = raw_echo.reshape(2, n_range, per_device, shard_samples)
    pieces = lax.all_to_all(grouped, "range", split_axis=1, concat_axis=3, tiled=True)
    real_out, imag_out = spectral(
        pieces[0].astype(jnp.float32), pieces[1].astype(jnp.float32), -1.0
    )
    spectrum = jnp.stack([real_out, imag_out]).astype(jnp.bfloat16)
    spectrum = spectrum.reshape(2, per_device, shard_samples * n_range)
    band_bins = spectrum.shape[2] // n_pulse
    first_pulse = my_range * per_device
    cols_here = lax.dynamic_slice_in_dim(tile_col[:, 0], first_pulse, per_device)
    taps_here = lax.dynamic_slice_in_dim(azim_taps, first_pulse, per_device, 0)
    position = jnp.arange(per_device, dtype=jnp.int32)
    earlier = position[None, :] < position[:, None]
    same_tile = cols_here[:, None] == cols_here[None, :]
    slot_rank = jnp.sum(jnp.where(earlier & same_tile, 1, 0), axis=1)
    tile_ids = jnp.arange(n_range, dtype=jnp.int32)
    slot_ids = jnp.arange(CAP, dtype=jnp.int32)
    placing = (
        (cols_here[None, None, :] == tile_ids[:, None, None])
        & (slot_rank[None, None, :] == slot_ids[None, :, None])
    ).astype(jnp.bfloat16)
    banded = spectrum.reshape(2, per_device, n_pulse, band_bins)
    send_lines = jnp.einsum(
        "tcq,xqpb->ptcxb", placing, banded, preferred_element_type=jnp.float32
    ).astype(jnp.bfloat16)
    send_taps = jnp.einsum(
        "tcq,qw->tcw", placing, taps_here, preferred_element_type=jnp.float32
    ).astype(jnp.bfloat16)
    tile_width = send_taps.shape[2]
    send_taps = jnp.broadcast_to(send_taps[None], (n_pulse, n_range, CAP, tile_width))
    block_count, block_bins, block_rows = range_taps.shape
    flat_lines = send_lines.reshape(n_pulse * n_range, CAP, 2, band_bins)
    flat_taps = send_taps.reshape(n_pulse * n_range, CAP, tile_width)
    line_block = lax.all_to_all(
        flat_lines, ("pulse", "range"), split_axis=0, concat_axis=0, tiled=True
    )
    tap_block = lax.all_to_all(
        flat_taps, ("pulse", "range"), split_axis=0, concat_axis=0, tiled=True
    )
    blocked = line_block.reshape(line_block.shape[:3] + (block_count, block_bins))
    resampled = jnp.einsum(
        "skxbr,brj->skxbj", blocked, range_taps, preferred_element_type=jnp.float32
    )
    ky_rows = resampled.reshape(line_block.shape[:3] + (block_count * block_rows,)).astype(
        jnp.bfloat16
    )
    band_rows = ky_rows.shape[3]
    slot_total = ky_rows.shape[0] * ky_rows.shape[1]
    slot_lines = ky_rows.reshape(slot_total, 2, band_rows)
    slot_taps = tap_block.reshape(slot_total, tile_width)
    half_width = tile_width // 2
    other_lines, other_taps = swapped((slot_lines, slot_taps), "sub", 0)
    column_start = my_sub * half_width
    my_taps = lax.dynamic_slice_in_dim(slot_taps, column_start, half_width, 1)
    their_taps = lax.dynamic_slice_in_dim(other_taps, column_start, half_width, 1)
    own_part = jnp.einsum("mi,mxj->xij", my_taps, slot_lines, preferred_element_type=jnp.float32)
    far_part = jnp.einsum(
        "mi,mxj->xij", their_taps, other_lines, preferred_element_type=jnp.float32
    )
    own_round = lax.optimization_barrier(own_part.astype(jnp.bfloat16))
    far_round = lax.optimization_barrier(far_part.astype(jnp.bfloat16))
    kspace = own_round.astype(jnp.float32) + far_round.astype(jnp.float32)
    pieces_each = half_width // n_pulse
    shaped = kspace.reshape(2, n_pulse, pieces_each, band_rows)
    pieces = lax.all_to_all(
        shaped.astype(jnp.bfloat16), "pulse", split_axis=1, concat_axis=3, tiled=True
    ).astype(shaped.dtype)
    real_out, imag_out = spectral(pieces[0], pieces[1], 1.0)
    columns_done = jnp.stack([real_out, imag_out])
    columns_done = columns_done.reshape(2, pieces_each, band_rows * n_pulse)
    moved = lax.all_to_all(
        lax.all_to_all(as_sent(columns_done), "pulse", split_axis=2, concat_axis=1, tiled=True),
        ("range", "sub"),
        split_axis=2,
        concat_axis=1,
        tiled=True,
    ).astype(columns_done.dtype)
    flipped = jnp.swapaxes(moved, 1, 2)
    real_out, imag_out = spectral(flipped[0], flipped[1], 1.0)
    return jnp.stack([real_out, imag_out])


LANES = 128
BF16 = jnp.bfloat16
F32 = jnp.float32
MESH = pl.DeviceIdType.MESH


def split_bf16(table):
    high = table.astype(ml_dtypes.bfloat16)
    low = (table - high.astype(np.float64)).astype(ml_dtypes.bfloat16)
    return np.stack([high, low])


def turn(fraction):
    return np.exp(2j * np.pi * (fraction % 1.0))


def pulse_tables(samples, n_range):
    rows = samples // LANES
    k = np.arange(LANES)
    first = turn(-np.outer(k, np.arange(rows)) / rows) / math.sqrt(samples)
    parts = first.reshape(LANES, n_range, rows // n_range)
    real = np.stack([parts.real, -parts.imag], axis=2).reshape(LANES, 2 * rows)
    imag = np.stack([parts.imag, parts.real], axis=2).reshape(LANES, 2 * rows)
    left = split_bf16(np.concatenate([real, imag]))
    second = turn(-np.outer(k, k) / LANES)
    right = split_bf16(np.block([[second.real, -second.imag], [second.imag, second.real]]))
    twist = turn(-np.outer(k, k) / samples)
    return left, right, np.stack([twist.real, twist.imag]).astype(np.float32)


def column_tables(grid, n_pulse, rows, devices):
    band = grid // n_pulse
    u = np.arange(grid).reshape(n_pulse, 1, band)
    angle = turn(u * np.arange(rows)[None, :, None] / grid) / math.sqrt(grid)
    table = np.concatenate([angle.real, angle.imag], axis=2).astype(ml_dtypes.bfloat16)
    shift = turn(np.outer(np.arange(devices) * rows, np.arange(LANES)) / grid)
    return table, np.stack([shift.real, shift.imag]).astype(np.float32)[:, :, None, :]


def row_tables(grid):
    upper = grid // LANES
    twist = turn(np.outer(np.arange(upper), np.arange(LANES)) / grid)
    k = np.arange(LANES)
    second = turn(np.outer(k, k) / LANES) / math.sqrt(grid)
    factor = np.concatenate([second.real, second.imag], axis=1).astype(ml_dtypes.bfloat16)
    return np.stack([twist.real, twist.imag], axis=1).astype(np.float32), factor


def plus(a, b):
    return b if a is None else a if b is None else a + b


def minus(a, b):
    if b is None:
        return a
    return -b if a is None else a - b


def plane_transform(real, imag):
    count = len(real)
    if count == 1:
        return real, imag
    even_r, even_i = plane_transform(real[0::2], imag[0::2])
    odd_r, odd_i = plane_transform(real[1::2], imag[1::2])
    low_r, low_i, high_r, high_i = [], [], [], []
    for k in range(count // 2):
        a, b = odd_r[k], odd_i[k]
        if k == 0:
            tr, ti = a, b
        elif 4 * k == count:
            tr, ti = minus(None, b), a
        else:
            c = math.cos(2.0 * math.pi * k / count)
            s = math.sin(2.0 * math.pi * k / count)
            tr, ti = a * c, a * s
            if b is not None:
                tr, ti = tr - b * s, ti + b * c
        low_r.append(plus(even_r[k], tr))
        low_i.append(plus(even_i[k], ti))
        high_r.append(minus(even_r[k], tr))
        high_i.append(minus(even_i[k], ti))
    return low_r + high_r, low_i + high_i


def matmul(a, b):
    return jnp.dot(a, b, preferred_element_type=F32)


def matmul_nt(a, b):
    return lax.dot_general(a, b, (((1,), (1,)), ((), ())), preferred_element_type=F32)


def form_kernel(
    sizes,
    raw_in, az_in, tile_ref, left_hbm, right_hbm, twist_hbm, shift_hbm, taps_hbm, phase_hbm, factor_hbm, coltab_hbm,
    lhs_ref, rhs_ref,
    left_ref, right_ref, twist_ref, shift_ref, taps_ref, phase_ref, factor_ref, raw_f32, raw_ref, x_buf, az_ref, az_buf, sp_out, sp_in, sp_f32, spun, rhs_f32, turned, col_buf, part_out, part_in, sums,
    table_sem, local_sem, x_send, x_recv, az_send, az_recv, sp_send, sp_recv, part_send, part_recv,
):
    n_pulse, n_range, n_sub = sizes
    devices = n_pulse * n_range * n_sub
    z, x, s = lax.axis_index("pulse"), lax.axis_index("range"), lax.axis_index("sub")
    me = (z * n_range + x) * n_sub + s
    shards = n_pulse * n_sub
    shard = z * n_sub + s
    pulses = x_buf.shape[2]
    blocks = taps_hbm.shape[0]
    band_rows = sp_in.shape[3]

    def whole_id(index):
        rest = index // n_sub
        return {"pulse": rest // n_range, "range": rest % n_range, "sub": index % n_sub}

    tables = [
        pltpu.make_async_copy(source, target, table_sem.at[i])
        for i, (source, target) in enumerate([
            (left_hbm, left_ref), (twist_hbm, twist_ref), (right_hbm, right_ref), (phase_hbm, phase_ref),
            (factor_hbm, factor_ref), (taps_hbm, taps_ref), (shift_hbm, shift_ref), (coltab_hbm.at[z], col_buf)])]
    left_copy, twist_copy, right_copy, phase_copy, factor_copy, taps_copy, shift_copy, table_copy = tables
    for copy in tables:
        copy.start()
    chunks = raw_ref.shape[2]
    shard_pulses = raw_ref.shape[1]
    for c in range(2):
        for j in range(chunks):
            rows = pl.ds(c * shard_pulses * chunks + j, shard_pulses, stride=chunks)
            raw_f32[rows, :] = raw_in[c, :, j * LANES:(j + 1) * LANES].astype(F32)
    raw_ref[...] = raw_f32[...].astype(BF16).reshape(raw_ref.shape)
    half_width = az_in.shape[1] // 2
    weights = az_in[...].astype(F32)
    sign = jnp.broadcast_to(1.0 - 2.0 * tile_ref[...].astype(F32), (shard_pulses, LANES))
    az_ref[:, 0:half_width] = jnp.concatenate([weights[:, :half_width], weights[:, half_width:]], axis=0).astype(BF16)
    az_ref[:, half_width:half_width + LANES] = jnp.concatenate([sign, sign], axis=0).astype(BF16)
    own_raw = pltpu.make_async_copy(raw_ref.at[:, pl.ds(x * pulses, pulses)], x_buf.at[x], local_sem.at[1])
    own_raw.start()
    own_az = pltpu.make_async_copy(az_ref, az_buf.at[shard], local_sem.at[2])
    own_az.start()

    barrier = pltpu.get_barrier_semaphore()
    for r in range(1, devices):
        pl.semaphore_signal(barrier, inc=1, device_id=whole_id((me + r) % devices), device_id_type=MESH)
    pl.semaphore_wait(barrier, devices - 1)

    raw_copies = []
    for r in range(1, n_range):
        other = (x + r) % n_range
        copy = pltpu.make_async_remote_copy(
            raw_ref.at[:, pl.ds(other * pulses, pulses)], x_buf.at[x], x_send.at[r], x_recv.at[r],
            device_id={"pulse": z, "range": other, "sub": s}, device_id_type=MESH)
        copy.start()
        raw_copies.append(copy)
    az_copies = []
    for r in range(1, shards):
        other = (shard + r) % shards
        copy = pltpu.make_async_remote_copy(
            az_ref, az_buf.at[shard], az_send.at[r], az_recv.at[r],
            device_id={"pulse": other // n_sub, "range": x, "sub": other % n_sub}, device_id_type=MESH)
        copy.start()
        az_copies.append(copy)

    own_raw.wait()
    for copy in raw_copies:
        copy.wait()

    left_copy.wait()
    twist_copy.wait()
    right_copy.wait()
    twist_r, twist_i = twist_ref[0], twist_ref[1]
    samples = jnp.concatenate(
        [jnp.concatenate([x_buf[h, c, p] for h in range(n_range) for c in range(2)], axis=0)
         for p in range(pulses)], axis=1)
    mixed = matmul(left_ref[0], samples) + matmul(left_ref[1], samples)
    both = []
    for p in range(pulses):
        lanes = slice(p * LANES, (p + 1) * LANES)
        mr, mi = mixed[:LANES, lanes], mixed[LANES:, lanes]
        both.append(jnp.concatenate([mr * twist_r - mi * twist_i, mr * twist_i + mi * twist_r], axis=1))
    both = jnp.concatenate(both, axis=0)
    high = both.astype(BF16)
    low = (both - high.astype(F32)).astype(BF16)
    bins = (matmul_nt(right_ref[0], high) + matmul_nt(right_ref[1], high)
            + matmul_nt(right_ref[0], low)).astype(BF16)
    for c in range(2):
        for d in range(n_pulse):
            for p in range(pulses):
                start = c * LANES + d * band_rows
                sp_out[d, c, p] = bins[start:start + band_rows, p * LANES:(p + 1) * LANES]
    own_bins = pltpu.make_async_copy(sp_out.at[z], sp_in.at[z], local_sem.at[1])
    own_bins.start()
    bin_copies = []
    for r in range(1, n_pulse):
        other = (z + r) % n_pulse
        copy = pltpu.make_async_remote_copy(
            sp_out.at[other], sp_in.at[z], sp_send.at[r], sp_recv.at[r],
            device_id={"pulse": other, "range": x, "sub": s}, device_id_type=MESH)
        copy.start()
        bin_copies.append(copy)

    own_az.wait()
    for copy in az_copies:
        copy.wait()
    phase_copy.wait()
    upper = phase_ref.shape[0]
    half = upper // 2
    total = shards * shard_pulses

    def row_step(i, carry):
        pair = [az_buf[2 * i].astype(F32), az_buf[2 * i + 1].astype(F32)]

        def piece(top, lane):
            return jnp.concatenate(
                [a[top * shard_pulses:(top + 1) * shard_pulses, lane:lane + LANES] for a in pair], axis=0)

        taps = [piece(c * LANES // half_width, c * LANES % half_width) for c in range(half)]
        signed = piece(0, half_width)
        rows = pl.ds(pl.multiple_of(2 * shard_pulses * i, 2 * shard_pulses), 2 * shard_pulses)
        rows_i = pl.ds(pl.multiple_of(total + 2 * shard_pulses * i, 2 * shard_pulses), 2 * shard_pulses)
        for parity in range(2):
            if parity == 0:
                real, imag = taps, [None] * half
            else:
                real = [t * signed * math.cos(2.0 * math.pi * c / upper) for c, t in enumerate(taps)]
                imag = [t * signed * math.sin(2.0 * math.pi * c / upper) for c, t in enumerate(taps)]
            real, imag = plane_transform(real, imag)
            for m in range(half):
                low = 2 * m + parity
                pr, pi = phase_ref[low, 0:1, :], phase_ref[low, 1:2, :]
                qr, qi = real[m] * pr, real[m] * pi
                if imag[m] is not None:
                    qr, qi = qr - imag[m] * pi, qi + imag[m] * pr
                qr, qi = qr.astype(BF16), qi.astype(BF16)
                spun[low, rows, 0:LANES] = qr
                spun[low, rows, LANES:2 * LANES] = -qi
                spun[low, rows_i, 0:LANES] = qi
                spun[low, rows_i, LANES:2 * LANES] = qr
        return carry

    lax.fori_loop(0, shards // 2, row_step, 0)
    own_bins.wait()
    for copy in bin_copies:
        copy.wait()
    lines = n_pulse * pulses
    taps_copy.wait()
    factor_copy.wait()
    shift_copy.wait()
    table_copy.wait()
    for d in range(n_pulse):
        for c in range(2):
            for p in range(pulses):
                at = ((c * n_pulse + d) * pulses + p) * band_rows
                sp_f32[at:at + band_rows] = sp_in[d, c, p].astype(F32)
    per_block = band_rows // blocks
    band = blocks * LANES
    shift_r, shift_i = shift_ref[0], shift_ref[1]
    for b in range(blocks):
        bins = jnp.concatenate(
            [sp_f32[pl.ds(b * per_block + q, 2 * lines, stride=band_rows), :] for q in range(per_block)], axis=1)
        line = matmul(bins.astype(BF16), taps_ref[b]).astype(BF16).astype(F32)
        kr, ki = line[None, :lines], line[None, lines:]
        tr = (kr * shift_r - ki * shift_i).astype(BF16)
        ti = (kr * shift_i + ki * shift_r).astype(BF16)
        lane = b * LANES
        turned[:, 0:lines, lane:lane + LANES] = tr
        turned[:, 0:lines, band + lane:band + lane + LANES] = -ti
        turned[:, lines:2 * lines, lane:lane + LANES] = ti
        turned[:, lines:2 * lines, band + lane:band + lane + LANES] = tr
    part = matmul_nt(turned[...].reshape(devices * 2 * lines, 2 * band), col_buf[...])
    part_out[...] = part.astype(BF16).reshape(part_out.shape)

    own_part = pltpu.make_async_copy(part_out.at[me], part_in.at[me], local_sem.at[1])
    own_part.start()
    part_copies = []
    for r in range(1, devices):
        other = (me + r) % devices
        copy = pltpu.make_async_remote_copy(
            part_out.at[other], part_in.at[me], part_send.at[r], part_recv.at[r],
            device_id=whole_id(other), device_id_type=MESH)
        copy.start()
        part_copies.append(copy)
    for low in range(upper):
        rhs_f32[pl.ds(low, LANES, stride=upper), :] = matmul_nt(factor_ref[...], spun[low])
    rhs_ref[...] = rhs_f32[...].astype(BF16)
    own_part.wait()
    for copy in part_copies:
        copy.wait()

    per_sub = n_range * n_sub
    out_rows = col_buf.shape[0]
    for k in range(per_sub):
        acc = part_in[k].astype(F32)
        for d in range(1, n_pulse):
            acc = acc + part_in[d * per_sub + k].astype(F32)
        xx, ss = k // n_sub, k % n_sub
        for c in range(2):
            for d in range(n_pulse):
                src = c * lines + d * pulses
                dst = c * total + ((d * n_sub + ss) * n_range + xx) * pulses
                sums[dst:dst + pulses, :] = acc[src:src + pulses]
    real = jnp.transpose(sums[0:total, :])
    imag = jnp.transpose(sums[total:2 * total, :])
    lhs_ref[0:out_rows, :] = jnp.concatenate([real, -imag], axis=1).astype(BF16)
    lhs_ref[out_rows:2 * out_rows, :] = jnp.concatenate([imag, real], axis=1).astype(BF16)


def image_kernel(lhs_ref, rhs_ref, out_ref):
    out_ref[...] = matmul_nt(lhs_ref[...], rhs_ref[...])


def low_rank_body(raw_echo, range_taps, azim_taps, tile_col):
    n_range, n_pulse, n_sub = lax.axis_size("range"), lax.axis_size("pulse"), lax.axis_size("sub")
    devices = n_range * n_pulse * n_sub
    shard_pulses, shard_samples = raw_echo.shape[1], raw_echo.shape[2]
    samples = shard_samples * n_range
    pulses = shard_pulses // n_range
    blocks, block_bins, block_rows = range_taps.shape
    grid = blocks * block_rows * n_pulse
    width = azim_taps.shape[1]
    rows = grid // devices
    total = shard_pulses * n_pulse * n_sub
    lines = n_pulse * pulses
    band_rows = samples // LANES // n_pulse

    left, right, twist = pulse_tables(samples, n_range)
    coltab, shift = column_tables(grid, n_pulse, rows, devices)
    phase, factor = row_tables(grid)

    vmem = pl.BlockSpec(memory_space=pltpu.VMEM)
    lhs, rhs = pl.pallas_call(
        functools.partial(form_kernel, (n_pulse, n_range, n_sub)),
        out_shape=(
            jax.ShapeDtypeStruct((2 * rows, 2 * total), BF16),
            jax.ShapeDtypeStruct((grid, 2 * total), BF16),
        ),
        in_specs=[vmem] * 3 + [pl.BlockSpec(memory_space=pltpu.HBM)] * 8,
        out_specs=(vmem, vmem),
        scratch_shapes=[
            pltpu.VMEM(left.shape, BF16),
            pltpu.VMEM(right.shape, BF16),
            pltpu.VMEM(twist.shape, F32),
            pltpu.VMEM(shift.shape, F32),
            pltpu.VMEM(range_taps.shape, BF16),
            pltpu.VMEM(phase.shape, F32),
            pltpu.VMEM(factor.shape, BF16),
            pltpu.VMEM((raw_echo.size // LANES, LANES), F32),
            pltpu.VMEM((2, shard_pulses, shard_samples // LANES, LANES), BF16),
            pltpu.VMEM((n_range, 2, pulses, shard_samples // LANES, LANES), BF16),
            pltpu.VMEM((2 * shard_pulses, width // 2 + LANES), BF16),
            pltpu.VMEM((n_pulse * n_sub, 2 * shard_pulses, width // 2 + LANES), BF16),
            pltpu.VMEM((n_pulse, 2, pulses, band_rows, LANES), BF16),
            pltpu.VMEM((n_pulse, 2, pulses, band_rows, LANES), BF16),
            pltpu.VMEM((2 * lines * band_rows, LANES), F32),
            pltpu.VMEM((grid // LANES, 2 * total, 2 * LANES), BF16),
            pltpu.VMEM((grid, 2 * total), F32),
            pltpu.VMEM((devices, 2 * lines, 2 * grid // n_pulse), BF16),
            pltpu.VMEM((rows, 2 * grid // n_pulse), BF16),
            pltpu.VMEM((devices, 2 * lines, rows), BF16),
            pltpu.VMEM((devices, 2 * lines, rows), BF16),
            pltpu.VMEM((2 * total, rows), F32),
            pltpu.SemaphoreType.DMA((8,)),
            pltpu.SemaphoreType.DMA((3,)),
            pltpu.SemaphoreType.DMA((n_range,)),
            pltpu.SemaphoreType.DMA((n_range,)),
            pltpu.SemaphoreType.DMA((n_pulse * n_sub,)),
            pltpu.SemaphoreType.DMA((n_pulse * n_sub,)),
            pltpu.SemaphoreType.DMA((n_pulse,)),
            pltpu.SemaphoreType.DMA((n_pulse,)),
            pltpu.SemaphoreType.DMA((devices,)),
            pltpu.SemaphoreType.DMA((devices,)),
        ],
        compiler_params=pltpu.CompilerParams(
            collective_id=0, has_side_effects=True, vmem_limit_bytes=60 * 2 ** 20),
    )(raw_echo, azim_taps, tile_col, left, right, twist, shift, range_taps, phase, factor, coltab)
    columns = min(grid, 4 * LANES)
    image = pl.pallas_call(
        image_kernel,
        grid=(grid // columns,),
        out_shape=jax.ShapeDtypeStruct((2 * rows, grid), F32),
        in_specs=[
            pl.BlockSpec((2 * rows, 2 * total), lambda i: (0, 0)),
            pl.BlockSpec((columns, 2 * total), lambda i: (i, 0)),
        ],
        out_specs=pl.BlockSpec((2 * rows, columns), lambda i: (0, i)),
        compiler_params=pltpu.CompilerParams(vmem_limit_bytes=60 * 2 ** 20),
    )(lhs, rhs)
    return image.reshape(2, rows, grid)


def body(raw_echo, range_taps, azim_taps, tile_col):
    n_range, n_pulse, n_sub = lax.axis_size("range"), lax.axis_size("pulse"), lax.axis_size("sub")
    samples = raw_echo.shape[2] * n_range
    grid = range_taps.shape[0] * range_taps.shape[2] * n_pulse
    pulses = raw_echo.shape[1] * n_pulse * n_sub
    band_rows = samples // LANES // n_pulse
    low_rank = 16 * pulses <= grid
    fits = (
        samples == LANES * LANES
        and grid // LANES * LANES == grid
        and azim_taps.shape[1] * 2 == grid
        and grid % (8 * LANES) == 0
        and range_taps.shape[2] == LANES
        and band_rows % 16 == 0
        and pulses % 16 == 0
        and raw_echo.shape[1] == 8
        and grid // (n_range * n_pulse * n_sub) % LANES == 0
    )
    if low_rank and fits:
        return low_rank_body(raw_echo, range_taps, azim_taps, tile_col)
    return general_body(raw_echo, range_taps, azim_taps, tile_col)


def solution(mesh):
    placed = (
        P(None, ("groups", "pulse", "sub"), "range"),
        P("pulse", None, None),
        P(("groups", "pulse", "sub"), None),
        P(("groups", "pulse", "sub"), None),
    )
    return jax.shard_map(
        body,
        mesh=mesh,
        in_specs=placed,
        out_specs=P(None, ("groups", "pulse", "range", "sub"), None),
        check_vma=False,
    )
```

```python
import functools
import math

import jax
import jax.numpy as jnp
import ml_dtypes
import numpy as np
from jax import lax
from jax.experimental import pallas as pl
from jax.experimental.pallas import tpu as pltpu
from jax.sharding import PartitionSpec as P

CAP = 2


def swapped(block, axis, bit):
    count = lax.axis_size(axis)
    route = []
    for low in range(count):
        high = low | 1 << bit
        if high != low and high < count:
            route += [(low, high), (high, low)]
    return lax.ppermute(block, axis, route)


def as_sent(value):
    return jax.tree.map(lambda a: a.astype(jnp.bfloat16) if a.dtype == jnp.float32 else a, value)


def tables(points, direction):
    indices = jnp.arange(points, dtype=jnp.int32)
    phases = indices[:, None] * indices[None, :] % points
    angles = phases.astype(jnp.float32) * (2.0 * math.pi / points)
    return (jnp.cos(angles), direction * jnp.sin(angles))


def spectral(real_part, imag_part, direction):
    length = real_part.shape[-1]
    outer_len = 1 << (length.bit_length() - 1) // 2
    inner_len = length // outer_len
    leading = real_part.shape[:-1]
    real_part = real_part.reshape(leading + (outer_len, inner_len))
    imag_part = imag_part.reshape(leading + (outer_len, inner_len))
    highest = lax.Precision.HIGHEST
    cos_outer, sin_outer = tables(outer_len, direction)
    mixed_real = jnp.einsum(
        "...nm,nk->...km", real_part, cos_outer, precision=highest
    ) - jnp.einsum("...nm,nk->...km", imag_part, sin_outer, precision=highest)
    mixed_imag = jnp.einsum(
        "...nm,nk->...km", real_part, sin_outer, precision=highest
    ) + jnp.einsum("...nm,nk->...km", imag_part, cos_outer, precision=highest)
    outer_index = jnp.arange(outer_len, dtype=jnp.int32)[:, None]
    inner_index = jnp.arange(inner_len, dtype=jnp.int32)[None, :]
    twists = (outer_index * inner_index % length).astype(jnp.float32) * (2.0 * math.pi / length)
    twist_cos = jnp.cos(twists)
    twist_sin = direction * jnp.sin(twists)
    turned_real = mixed_real * twist_cos - mixed_imag * twist_sin
    turned_imag = mixed_real * twist_sin + mixed_imag * twist_cos
    cos_inner, sin_inner = tables(inner_len, direction)
    final_real = jnp.einsum(
        "...km,mj->...jk", turned_real, cos_inner, precision=highest
    ) - jnp.einsum("...km,mj->...jk", turned_imag, sin_inner, precision=highest)
    final_imag = jnp.einsum(
        "...km,mj->...jk", turned_real, sin_inner, precision=highest
    ) + jnp.einsum("...km,mj->...jk", turned_imag, cos_inner, precision=highest)
    norm_scale = 1.0 / math.sqrt(length)
    return (
        (final_real * norm_scale).reshape(leading + (length,)),
        (final_imag * norm_scale).reshape(leading + (length,)),
    )


def general_body(raw_echo, range_taps, azim_taps, tile_col):
    n_range = lax.axis_size("range")
    n_pulse = lax.axis_size("pulse")
    my_range = lax.axis_index("range")
    my_sub = lax.axis_index("sub")
    shard_pulses = raw_echo.shape[1]
    shard_samples = raw_echo.shape[2]
    per_device = shard_pulses // n_range
    grouped = raw_echo.reshape(2, n_range, per_device, shard_samples)
    pieces = lax.all_to_all(grouped, "range", split_axis=1, concat_axis=3, tiled=True)
    real_out, imag_out = spectral(
        pieces[0].astype(jnp.float32), pieces[1].astype(jnp.float32), -1.0
    )
    spectrum = jnp.stack([real_out, imag_out]).astype(jnp.bfloat16)
    spectrum = spectrum.reshape(2, per_device, shard_samples * n_range)
    band_bins = spectrum.shape[2] // n_pulse
    first_pulse = my_range * per_device
    cols_here = lax.dynamic_slice_in_dim(tile_col[:, 0], first_pulse, per_device)
    taps_here = lax.dynamic_slice_in_dim(azim_taps, first_pulse, per_device, 0)
    position = jnp.arange(per_device, dtype=jnp.int32)
    earlier = position[None, :] < position[:, None]
    same_tile = cols_here[:, None] == cols_here[None, :]
    slot_rank = jnp.sum(jnp.where(earlier & same_tile, 1, 0), axis=1)
    tile_ids = jnp.arange(n_range, dtype=jnp.int32)
    slot_ids = jnp.arange(CAP, dtype=jnp.int32)
    placing = (
        (cols_here[None, None, :] == tile_ids[:, None, None])
        & (slot_rank[None, None, :] == slot_ids[None, :, None])
    ).astype(jnp.bfloat16)
    banded = spectrum.reshape(2, per_device, n_pulse, band_bins)
    send_lines = jnp.einsum(
        "tcq,xqpb->ptcxb", placing, banded, preferred_element_type=jnp.float32
    ).astype(jnp.bfloat16)
    send_taps = jnp.einsum(
        "tcq,qw->tcw", placing, taps_here, preferred_element_type=jnp.float32
    ).astype(jnp.bfloat16)
    tile_width = send_taps.shape[2]
    send_taps = jnp.broadcast_to(send_taps[None], (n_pulse, n_range, CAP, tile_width))
    block_count, block_bins, block_rows = range_taps.shape
    flat_lines = send_lines.reshape(n_pulse * n_range, CAP, 2, band_bins)
    flat_taps = send_taps.reshape(n_pulse * n_range, CAP, tile_width)
    line_block = lax.all_to_all(
        flat_lines, ("pulse", "range"), split_axis=0, concat_axis=0, tiled=True
    )
    tap_block = lax.all_to_all(
        flat_taps, ("pulse", "range"), split_axis=0, concat_axis=0, tiled=True
    )
    blocked = line_block.reshape(line_block.shape[:3] + (block_count, block_bins))
    resampled = jnp.einsum(
        "skxbr,brj->skxbj", blocked, range_taps, preferred_element_type=jnp.float32
    )
    ky_rows = resampled.reshape(line_block.shape[:3] + (block_count * block_rows,)).astype(
        jnp.bfloat16
    )
    band_rows = ky_rows.shape[3]
    slot_total = ky_rows.shape[0] * ky_rows.shape[1]
    slot_lines = ky_rows.reshape(slot_total, 2, band_rows)
    slot_taps = tap_block.reshape(slot_total, tile_width)
    half_width = tile_width // 2
    other_lines, other_taps = swapped((slot_lines, slot_taps), "sub", 0)
    column_start = my_sub * half_width
    my_taps = lax.dynamic_slice_in_dim(slot_taps, column_start, half_width, 1)
    their_taps = lax.dynamic_slice_in_dim(other_taps, column_start, half_width, 1)
    own_part = jnp.einsum("mi,mxj->xij", my_taps, slot_lines, preferred_element_type=jnp.float32)
    far_part = jnp.einsum(
        "mi,mxj->xij", their_taps, other_lines, preferred_element_type=jnp.float32
    )
    own_round = lax.optimization_barrier(own_part.astype(jnp.bfloat16))
    far_round = lax.optimization_barrier(far_part.astype(jnp.bfloat16))
    kspace = own_round.astype(jnp.float32) + far_round.astype(jnp.float32)
    pieces_each = half_width // n_pulse
    shaped = kspace.reshape(2, n_pulse, pieces_each, band_rows)
    pieces = lax.all_to_all(
        shaped.astype(jnp.bfloat16), "pulse", split_axis=1, concat_axis=3, tiled=True
    ).astype(shaped.dtype)
    real_out, imag_out = spectral(pieces[0], pieces[1], 1.0)
    columns_done = jnp.stack([real_out, imag_out])
    columns_done = columns_done.reshape(2, pieces_each, band_rows * n_pulse)
    moved = lax.all_to_all(
        lax.all_to_all(as_sent(columns_done), "pulse", split_axis=2, concat_axis=1, tiled=True),
        ("range", "sub"),
        split_axis=2,
        concat_axis=1,
        tiled=True,
    ).astype(columns_done.dtype)
    flipped = jnp.swapaxes(moved, 1, 2)
    real_out, imag_out = spectral(flipped[0], flipped[1], 1.0)
    return jnp.stack([real_out, imag_out])


LANES = 128
BF16 = jnp.bfloat16
F32 = jnp.float32
MESH = pl.DeviceIdType.MESH


def split_bf16(table):
    high = table.astype(ml_dtypes.bfloat16)
    low = (table - high.astype(np.float64)).astype(ml_dtypes.bfloat16)
    return np.stack([high, low])


def turn(fraction):
    return np.exp(2j * np.pi * (fraction % 1.0))


def pulse_tables(samples, n_range):
    rows = samples // LANES
    k = np.arange(LANES)
    first = turn(-np.outer(k, np.arange(rows)) / rows) / math.sqrt(samples)
    parts = first.reshape(LANES, n_range, rows // n_range)
    real = np.stack([parts.real, -parts.imag], axis=2).reshape(LANES, 2 * rows)
    imag = np.stack([parts.imag, parts.real], axis=2).reshape(LANES, 2 * rows)
    left = split_bf16(np.concatenate([real, imag]))
    second = turn(-np.outer(k, k) / LANES)
    right = split_bf16(np.block([[second.real, -second.imag], [second.imag, second.real]]))
    twist = turn(-np.outer(k, k) / samples)
    return left, right, np.stack([twist.real, twist.imag]).astype(np.float32)


def column_tables(grid, n_pulse, rows, devices):
    band = grid // n_pulse
    u = np.arange(grid).reshape(n_pulse, 1, band)
    angle = turn(u * np.arange(rows)[None, :, None] / grid) / math.sqrt(grid)
    table = np.concatenate([angle.real, angle.imag], axis=2).astype(ml_dtypes.bfloat16)
    shift = turn(np.outer(np.arange(devices) * rows, np.arange(LANES)) / grid)
    return table, np.stack([shift.real, shift.imag]).astype(np.float32)[:, :, None, :]


def row_tables(grid):
    upper = grid // LANES
    twist = turn(np.outer(np.arange(upper), np.arange(LANES)) / grid)
    k = np.arange(LANES)
    second = turn(np.outer(k, k) / LANES) / math.sqrt(grid)
    factor = np.concatenate([second.real, second.imag], axis=1).astype(ml_dtypes.bfloat16)
    return np.stack([twist.real, twist.imag], axis=1).astype(np.float32), factor


def plus(a, b):
    return b if a is None else a if b is None else a + b


def minus(a, b):
    if b is None:
        return a
    return -b if a is None else a - b


def plane_transform(real, imag):
    count = len(real)
    if count == 1:
        return real, imag
    even_r, even_i = plane_transform(real[0::2], imag[0::2])
    odd_r, odd_i = plane_transform(real[1::2], imag[1::2])
    low_r, low_i, high_r, high_i = [], [], [], []
    for k in range(count // 2):
        a, b = odd_r[k], odd_i[k]
        if k == 0:
            tr, ti = a, b
        elif 4 * k == count:
            tr, ti = minus(None, b), a
        else:
            c = math.cos(2.0 * math.pi * k / count)
            s = math.sin(2.0 * math.pi * k / count)
            tr, ti = a * c, a * s
            if b is not None:
                tr, ti = tr - b * s, ti + b * c
        low_r.append(plus(even_r[k], tr))
        low_i.append(plus(even_i[k], ti))
        high_r.append(minus(even_r[k], tr))
        high_i.append(minus(even_i[k], ti))
    return low_r + high_r, low_i + high_i


def matmul(a, b):
    return jnp.dot(a, b, preferred_element_type=F32)


def matmul_nt(a, b):
    return lax.dot_general(a, b, (((1,), (1,)), ((), ())), preferred_element_type=F32)


def form_kernel(
    sizes,
    raw_in, az_in, tile_ref, left_hbm, right_hbm, twist_hbm, shift_hbm, taps_hbm, phase_hbm, factor_hbm, coltab_hbm,
    lhs_ref, rhs_ref,
    left_ref, right_ref, twist_ref, shift_ref, taps_ref, phase_ref, factor_ref, raw_f32, raw_ref, x_buf, az_ref, az_buf, sp_out, sp_in, sp_f32, spun, rhs_f32, turned, col_buf, part_out, part_in, sums,
    table_sem, local_sem, x_send, x_recv, az_send, az_recv, sp_send, sp_recv, part_send, part_recv,
):
    n_pulse, n_range, n_sub = sizes
    devices = n_pulse * n_range * n_sub
    z, x, s = lax.axis_index("pulse"), lax.axis_index("range"), lax.axis_index("sub")
    me = (z * n_range + x) * n_sub + s
    shards = n_pulse * n_sub
    pulses = x_buf.shape[2]
    blocks = taps_hbm.shape[0]
    band_rows = sp_in.shape[3]

    def whole_id(index):
        rest = index // n_sub
        return {"pulse": rest // n_range, "range": rest % n_range, "sub": index % n_sub}

    tables = [
        pltpu.make_async_copy(source, target, table_sem.at[i])
        for i, (source, target) in enumerate([
            (left_hbm, left_ref), (twist_hbm, twist_ref), (right_hbm, right_ref), (phase_hbm, phase_ref),
            (factor_hbm, factor_ref), (taps_hbm, taps_ref), (shift_hbm, shift_ref), (coltab_hbm.at[z], col_buf)])]
    left_copy, twist_copy, right_copy, phase_copy, factor_copy, taps_copy, shift_copy, table_copy = tables
    for copy in tables:
        copy.start()
    chunks = raw_ref.shape[2]
    shard_pulses = raw_ref.shape[1]
    for c in range(2):
        for j in range(chunks):
            rows = pl.ds(c * shard_pulses * chunks + j, shard_pulses, stride=chunks)
            raw_f32[rows, :] = raw_in[c, :, j * LANES:(j + 1) * LANES].astype(F32)
    raw_ref[...] = raw_f32[...].astype(BF16).reshape(raw_ref.shape)
    half_width = az_in.shape[1] // 2
    weights = az_in[...].astype(F32)
    square = (shard_pulses, shard_pulses)
    diagonal = lax.broadcasted_iota(jnp.int32, square, 0) == lax.broadcasted_iota(jnp.int32, square, 1)
    tiles = jnp.broadcast_to(tile_ref[...].astype(F32), square)
    tiles = jnp.sum(jnp.where(diagonal, tiles, 0.0), axis=1, keepdims=True)
    sign = jnp.broadcast_to(1.0 - 2.0 * tiles, (shard_pulses, LANES))
    az_ref[:, 0:half_width] = jnp.concatenate([weights[:, :half_width], weights[:, half_width:]], axis=0).astype(BF16)
    az_ref[:, half_width:half_width + LANES] = jnp.concatenate([sign, sign], axis=0).astype(BF16)
    own_raw = pltpu.make_async_copy(raw_ref.at[:, pl.ds(x * pulses, pulses)], x_buf.at[x], local_sem.at[1])
    own_raw.start()
    own_az = pltpu.make_async_copy(az_ref, az_buf.at[s, z], local_sem.at[2])
    own_az.start()

    barrier = pltpu.get_barrier_semaphore()
    for r in range(1, devices):
        pl.semaphore_signal(barrier, inc=1, device_id=whole_id((me + r) % devices), device_id_type=MESH)
    pl.semaphore_wait(barrier, devices - 1)

    raw_copies = []
    for r in range(1, n_range):
        other = (x + r) % n_range
        copy = pltpu.make_async_remote_copy(
            raw_ref.at[:, pl.ds(other * pulses, pulses)], x_buf.at[x], x_send.at[r], x_recv.at[r],
            device_id={"pulse": z, "range": other, "sub": s}, device_id_type=MESH)
        copy.start()
        raw_copies.append(copy)
    az_copies = []
    for r in range(1, n_pulse):
        copy = pltpu.make_async_remote_copy(
            az_ref, az_buf.at[s, z], az_send.at[r], az_recv.at[r],
            device_id={"pulse": (z + r) % n_pulse, "range": x, "sub": s}, device_id_type=MESH)
        copy.start()
        az_copies.append(copy)

    own_raw.wait()
    for copy in raw_copies:
        copy.wait()

    left_copy.wait()
    twist_copy.wait()
    right_copy.wait()
    twist_r, twist_i = twist_ref[0], twist_ref[1]
    samples = jnp.concatenate(
        [jnp.concatenate([x_buf[h, c, p] for h in range(n_range) for c in range(2)], axis=0)
         for p in range(pulses)], axis=1)
    mixed = matmul(left_ref[0], samples) + matmul(left_ref[1], samples)
    both = []
    for p in range(pulses):
        lanes = slice(p * LANES, (p + 1) * LANES)
        mr, mi = mixed[:LANES, lanes], mixed[LANES:, lanes]
        both.append(jnp.concatenate([mr * twist_r - mi * twist_i, mr * twist_i + mi * twist_r], axis=1))
    both = jnp.concatenate(both, axis=0)
    high = both.astype(BF16)
    low = (both - high.astype(F32)).astype(BF16)
    bins = (matmul_nt(right_ref[0], high) + matmul_nt(right_ref[1], high)
            + matmul_nt(right_ref[0], low)).astype(BF16)
    for c in range(2):
        for d in range(n_pulse):
            for p in range(pulses):
                start = c * LANES + d * band_rows
                sp_out[d, c, p] = bins[start:start + band_rows, p * LANES:(p + 1) * LANES]
    own_bins = pltpu.make_async_copy(sp_out.at[z], sp_in.at[z], local_sem.at[1])
    own_bins.start()
    bin_copies = []
    for r in range(1, n_pulse):
        other = (z + r) % n_pulse
        copy = pltpu.make_async_remote_copy(
            sp_out.at[other], sp_in.at[z], sp_send.at[r], sp_recv.at[r],
            device_id={"pulse": other, "range": x, "sub": s}, device_id_type=MESH)
        copy.start()
        bin_copies.append(copy)

    own_az.wait()
    for copy in az_copies:
        copy.wait()
    core_copy = pltpu.make_async_remote_copy(
        az_buf.at[s], az_buf.at[s], az_send.at[0], az_recv.at[0],
        device_id={"pulse": z, "range": x, "sub": 1 - s}, device_id_type=MESH)
    core_copy.start()
    core_copy.wait()
    phase_copy.wait()
    upper = phase_ref.shape[0]
    half = upper // 2
    total = shards * shard_pulses

    def row_step(i, carry):
        pair = [az_buf[0, i].astype(F32), az_buf[1, i].astype(F32)]

        def piece(top, lane):
            return jnp.concatenate(
                [a[top * shard_pulses:(top + 1) * shard_pulses, lane:lane + LANES] for a in pair], axis=0)

        taps = [piece(c * LANES // half_width, c * LANES % half_width) for c in range(half)]
        signed = piece(0, half_width)
        rows = pl.ds(pl.multiple_of(2 * shard_pulses * i, 2 * shard_pulses), 2 * shard_pulses)
        rows_i = pl.ds(pl.multiple_of(total + 2 * shard_pulses * i, 2 * shard_pulses), 2 * shard_pulses)
        for parity in range(2):
            if parity == 0:
                real, imag = taps, [None] * half
            else:
                real = [t * signed * math.cos(2.0 * math.pi * c / upper) for c, t in enumerate(taps)]
                imag = [t * signed * math.sin(2.0 * math.pi * c / upper) for c, t in enumerate(taps)]
            real, imag = plane_transform(real, imag)
            for m in range(half):
                low = 2 * m + parity
                pr, pi = phase_ref[low, 0:1, :], phase_ref[low, 1:2, :]
                qr, qi = real[m] * pr, real[m] * pi
                if imag[m] is not None:
                    qr, qi = qr - imag[m] * pi, qi + imag[m] * pr
                qr, qi = qr.astype(BF16), qi.astype(BF16)
                spun[low, rows, 0:LANES] = qr
                spun[low, rows, LANES:2 * LANES] = -qi
                spun[low, rows_i, 0:LANES] = qi
                spun[low, rows_i, LANES:2 * LANES] = qr
        return carry

    lax.fori_loop(0, shards // 2, row_step, 0)
    own_bins.wait()
    for copy in bin_copies:
        copy.wait()
    lines = n_pulse * pulses
    taps_copy.wait()
    factor_copy.wait()
    shift_copy.wait()
    table_copy.wait()
    for d in range(n_pulse):
        for c in range(2):
            for p in range(pulses):
                at = ((c * n_pulse + d) * pulses + p) * band_rows
                sp_f32[at:at + band_rows] = sp_in[d, c, p].astype(F32)
    per_block = band_rows // blocks
    band = blocks * LANES
    shift_r, shift_i = shift_ref[0], shift_ref[1]
    for b in range(blocks):
        bins = jnp.concatenate(
            [sp_f32[pl.ds(b * per_block + q, 2 * lines, stride=band_rows), :] for q in range(per_block)], axis=1)
        line = matmul(bins.astype(BF16), taps_ref[b]).astype(BF16).astype(F32)
        kr, ki = line[None, :lines], line[None, lines:]
        tr = (kr * shift_r - ki * shift_i).astype(BF16)
        ti = (kr * shift_i + ki * shift_r).astype(BF16)
        lane = b * LANES
        turned[:, 0:lines, lane:lane + LANES] = tr
        turned[:, 0:lines, band + lane:band + lane + LANES] = -ti
        turned[:, lines:2 * lines, lane:lane + LANES] = ti
        turned[:, lines:2 * lines, band + lane:band + lane + LANES] = tr
    part = matmul_nt(turned[...].reshape(devices * 2 * lines, 2 * band), col_buf[...])
    part_out[...] = part.astype(BF16).reshape(part_out.shape)

    own_part = pltpu.make_async_copy(part_out.at[me], part_in.at[me], local_sem.at[1])
    own_part.start()
    part_copies = []
    for r in range(1, devices):
        other = (me + r) % devices
        copy = pltpu.make_async_remote_copy(
            part_out.at[other], part_in.at[me], part_send.at[r], part_recv.at[r],
            device_id=whole_id(other), device_id_type=MESH)
        copy.start()
        part_copies.append(copy)
    for low in range(upper):
        rhs_f32[pl.ds(low, LANES, stride=upper), :] = matmul_nt(factor_ref[...], spun[low])
    rhs_ref[...] = rhs_f32[...].astype(BF16)
    own_part.wait()
    for copy in part_copies:
        copy.wait()

    per_sub = n_range * n_sub
    out_rows = col_buf.shape[0]
    for k in range(per_sub):
        acc = part_in[k].astype(F32)
        for d in range(1, n_pulse):
            acc = acc + part_in[d * per_sub + k].astype(F32)
        xx, ss = k // n_sub, k % n_sub
        for c in range(2):
            for d in range(n_pulse):
                src = c * lines + d * pulses
                dst = c * total + ((d * n_sub + ss) * n_range + xx) * pulses
                sums[dst:dst + pulses, :] = acc[src:src + pulses]
    real = jnp.transpose(sums[0:total, :])
    imag = jnp.transpose(sums[total:2 * total, :])
    lhs_ref[0:out_rows, :] = jnp.concatenate([real, -imag], axis=1).astype(BF16)
    lhs_ref[out_rows:2 * out_rows, :] = jnp.concatenate([imag, real], axis=1).astype(BF16)


def image_kernel(lhs_ref, rhs_ref, out_ref):
    for start in range(0, rhs_ref.shape[0], 4 * LANES):
        columns = slice(start, start + 4 * LANES)
        out_ref[:, columns] = matmul_nt(lhs_ref[...], rhs_ref[columns])


def low_rank_body(raw_echo, range_taps, azim_taps, tile_col):
    n_range, n_pulse, n_sub = lax.axis_size("range"), lax.axis_size("pulse"), lax.axis_size("sub")
    devices = n_range * n_pulse * n_sub
    shard_pulses, shard_samples = raw_echo.shape[1], raw_echo.shape[2]
    samples = shard_samples * n_range
    pulses = shard_pulses // n_range
    blocks, block_bins, block_rows = range_taps.shape
    grid = blocks * block_rows * n_pulse
    width = azim_taps.shape[1]
    rows = grid // devices
    total = shard_pulses * n_pulse * n_sub
    lines = n_pulse * pulses
    band_rows = samples // LANES // n_pulse

    left, right, twist = pulse_tables(samples, n_range)
    coltab, shift = column_tables(grid, n_pulse, rows, devices)
    phase, factor = row_tables(grid)

    vmem = pl.BlockSpec(memory_space=pltpu.VMEM)
    lhs, rhs = pl.pallas_call(
        functools.partial(form_kernel, (n_pulse, n_range, n_sub)),
        out_shape=(
            jax.ShapeDtypeStruct((2 * rows, 2 * total), BF16),
            jax.ShapeDtypeStruct((grid, 2 * total), BF16),
        ),
        in_specs=[vmem] * 3 + [pl.BlockSpec(memory_space=pltpu.HBM)] * 8,
        out_specs=(vmem, vmem),
        scratch_shapes=[
            pltpu.VMEM(left.shape, BF16),
            pltpu.VMEM(right.shape, BF16),
            pltpu.VMEM(twist.shape, F32),
            pltpu.VMEM(shift.shape, F32),
            pltpu.VMEM(range_taps.shape, BF16),
            pltpu.VMEM(phase.shape, F32),
            pltpu.VMEM(factor.shape, BF16),
            pltpu.VMEM((raw_echo.size // LANES, LANES), F32),
            pltpu.VMEM((2, shard_pulses, shard_samples // LANES, LANES), BF16),
            pltpu.VMEM((n_range, 2, pulses, shard_samples // LANES, LANES), BF16),
            pltpu.VMEM((2 * shard_pulses, width // 2 + LANES), BF16),
            pltpu.VMEM((n_sub, n_pulse, 2 * shard_pulses, width // 2 + LANES), BF16),
            pltpu.VMEM((n_pulse, 2, pulses, band_rows, LANES), BF16),
            pltpu.VMEM((n_pulse, 2, pulses, band_rows, LANES), BF16),
            pltpu.VMEM((2 * lines * band_rows, LANES), F32),
            pltpu.VMEM((grid // LANES, 2 * total, 2 * LANES), BF16),
            pltpu.VMEM((grid, 2 * total), F32),
            pltpu.VMEM((devices, 2 * lines, 2 * grid // n_pulse), BF16),
            pltpu.VMEM((rows, 2 * grid // n_pulse), BF16),
            pltpu.VMEM((devices, 2 * lines, rows), BF16),
            pltpu.VMEM((devices, 2 * lines, rows), BF16),
            pltpu.VMEM((2 * total, rows), F32),
            pltpu.SemaphoreType.DMA((8,)),
            pltpu.SemaphoreType.DMA((3,)),
            pltpu.SemaphoreType.DMA((n_range,)),
            pltpu.SemaphoreType.DMA((n_range,)),
            pltpu.SemaphoreType.DMA((n_pulse,)),
            pltpu.SemaphoreType.DMA((n_pulse,)),
            pltpu.SemaphoreType.DMA((n_pulse,)),
            pltpu.SemaphoreType.DMA((n_pulse,)),
            pltpu.SemaphoreType.DMA((devices,)),
            pltpu.SemaphoreType.DMA((devices,)),
        ],
        compiler_params=pltpu.CompilerParams(
            collective_id=0, has_side_effects=True, vmem_limit_bytes=60 * 2 ** 20),
    )(raw_echo, azim_taps, tile_col.reshape(1, shard_pulses), left, right, twist, shift, range_taps, phase, factor, coltab)
    step_rows = min(rows, LANES)
    image = pl.pallas_call(
        image_kernel,
        grid=(2 * rows // step_rows,),
        out_shape=jax.ShapeDtypeStruct((2 * rows, grid), F32),
        in_specs=[
            pl.BlockSpec((step_rows, 2 * total), lambda i: (i, 0)),
            pl.BlockSpec((grid, 2 * total), lambda i: (0, 0)),
        ],
        out_specs=pl.BlockSpec((step_rows, grid), lambda i: (i, 0)),
        compiler_params=pltpu.CompilerParams(vmem_limit_bytes=60 * 2 ** 20),
    )(lhs, rhs)
    return image.reshape(2, rows, grid)


def body(raw_echo, range_taps, azim_taps, tile_col):
    n_range, n_pulse, n_sub = lax.axis_size("range"), lax.axis_size("pulse"), lax.axis_size("sub")
    samples = raw_echo.shape[2] * n_range
    grid = range_taps.shape[0] * range_taps.shape[2] * n_pulse
    pulses = raw_echo.shape[1] * n_pulse * n_sub
    band_rows = samples // LANES // n_pulse
    low_rank = 16 * pulses <= grid
    fits = (
        samples == LANES * LANES
        and grid // LANES * LANES == grid
        and azim_taps.shape[1] * 2 == grid
        and grid % (8 * LANES) == 0
        and range_taps.shape[2] == LANES
        and band_rows % 16 == 0
        and pulses % 16 == 0
        and raw_echo.shape[1] == 8
        and n_sub == 2
        and grid // (n_range * n_pulse * n_sub) % LANES == 0
    )
    if low_rank and fits:
        return low_rank_body(raw_echo, range_taps, azim_taps, tile_col)
    return general_body(raw_echo, range_taps, azim_taps, tile_col)


def solution(mesh):
    placed = (
        P(None, ("groups", "pulse", "sub"), "range"),
        P("pulse", None, None),
        P(("groups", "pulse", "sub"), None),
        P(("groups", "pulse", "sub"), None),
    )
    return jax.shard_map(
        body,
        mesh=mesh,
        in_specs=placed,
        out_specs=P(None, ("groups", "pulse", "range", "sub"), None),
        check_vma=False,
    )
```
